32 devices in a mesh: frame: 4 (over y, core), row: 4 (over z), col: 2 (over x).
Axes of the slice: x: 2, y: 2, z: 4, core: 2. Of those that a mesh axis runs over, the one named last changes fastest.
Arguments:
- queries: bfloat16 [4, 4, 2, 384, 256], P('frame', 'row', 'col'), may hold values from -8 to 8
- key_vectors: bfloat16 [4, 4, 2, 384, 256], P('frame', 'row', 'col'), may hold values from -8 to 8
- value_vectors: bfloat16 [4, 4, 2, 384, 256], P('frame', 'row', 'col'), may hold values from -6 to 6
- forward_out: bfloat16 [4, 4, 2, 384, 256], P('frame', 'row', 'col'), may hold values from -6 to 6
- cotangent: bfloat16 [4, 4, 2, 384, 256], P('frame', 'row', 'col'), may hold values from -48 to 48
- log_norm: float32 [4, 4, 2, 2, 384], P('frame', 'row', 'col'), may hold values from 5 to 14
Outputs:
- grad_queries: bfloat16 [4, 4, 2, 384, 256], P('frame', 'row', 'col')
- grad_keys: bfloat16 [4, 4, 2, 384, 256], P('frame', 'row', 'col')
- grad_values: bfloat16 [4, 4, 2, 384, 256], P('frame', 'row', 'col')
The draws below stay inside these ranges and needn't reach their ends.
All inputs are finite; a program needn't handle non-finite values.
Results may differ from the reference program's by a relative error of at most 0.006.
Values may be sent and summed in bfloat16 or wider, within the bound.
A program may use at most 128 MiB of HBM per device.

```python
import jax
import jax.numpy as jnp
from jax import lax

HEADS = 2
TILE_F = 6
TILE_R = 8
TILE_C = 8
TILE_TOK = 384
WIDTH = 256
TILES_F = 4
TILES_R = 4
TILES_C = 2


def draw_log_norm(key, part):
    key = jax.random.fold_in(key, 11)
    tile_count = TILE_F * TILE_R * TILE_C
    centre = jnp.log(jnp.float32(27 * tile_count)) + 1.9
    shape = (TILES_F, TILES_R, TILES_C, HEADS, tile_count)
    return centre + jax.random.uniform(key, shape, jnp.float32, -1.0, 0.6)


def level_of(key, extent, cuts, smallest, high):
    level, own = 1.0, jax.random.fold_in(key, 6)
    for axis_at, shards_of in cuts:
        heights = jnp.exp(jax.random.uniform(jax.random.fold_in(own, axis_at), (shards_of,), jnp.float32, smallest / len(cuts), high / len(cuts)))
        level = level * jnp.repeat(heights, extent[axis_at] // shards_of).reshape([-1 if axis == axis_at else 1 for axis in range(len(extent))])
    return level


def noise(key, dims, scale, most, cuts=(), kind=jnp.bfloat16):
    result = jax.random.normal(key, dims, jnp.float32) * scale
    if len(cuts) > 0:
        result = level_of(key, dims, cuts, -0.22, 0.18) * result
    return jnp.clip(result, min=-most, max=most).astype(kind)


def setup_inputs(seed: int = 0) -> dict:
    seeds = jax.random.split(jax.random.key(seed), 7)
    return {
        "queries": noise(seeds[0], (TILES_F, TILES_R, TILES_C, TILE_TOK, WIDTH), 1.4, 8.0, ((0, 4), (1, 4), (2, 2))),
        "key_vectors": noise(seeds[1], (TILES_F, TILES_R, TILES_C, TILE_TOK, WIDTH), 1.4, 8.0, ((0, 4), (1, 4), (2, 2))),
        "value_vectors": noise(seeds[2], (TILES_F, TILES_R, TILES_C, TILE_TOK, WIDTH), 1.0, 6.0, ((0, 4), (1, 4), (2, 2))),
        "forward_out": noise(seeds[3], (TILES_F, TILES_R, TILES_C, TILE_TOK, WIDTH), 1.0, 6.0, ((0, 4), (1, 4), (2, 2))),
        "cotangent": noise(seeds[4], (TILES_F, TILES_R, TILES_C, TILE_TOK, WIDTH), 8.0, 48.0, ((0, 4), (1, 4), (2, 2))),
        "log_norm": draw_log_norm(jax.random.fold_in(seeds[6], 71), 0),
    }


def rounded(values_in):
    return lax.optimization_barrier(values_in.astype(jnp.bfloat16)).astype(jnp.float32)


def neighbours(padded, frame_at, row_at, col_at):
    starts = [frame_at, row_at, col_at] + [jnp.int32(0)] * (padded.ndim - 3)
    block = lax.dynamic_slice(padded, starts, (3, 3, 3) + padded.shape[3:])
    return block.reshape((27 * padded.shape[3],) + padded.shape[4:])


def window_valid(frame_at, row_at, col_at, tiles_f, tiles_r, tiles_c):
    offsets = jnp.arange(3, dtype=jnp.int32) - 1
    along_f = (frame_at + offsets >= 0) & (frame_at + offsets < tiles_f)
    along_r = (row_at + offsets >= 0) & (row_at + offsets < tiles_r)
    along_c = (col_at + offsets >= 0) & (col_at + offsets < tiles_c)
    joined = along_f[:, None, None] & along_r[None, :, None] & along_c[None, None, :]
    return joined.reshape(27)


def reference(queries, key_vectors, value_vectors, forward_out, cotangent, log_norm):
    tiles_f, tiles_r, tiles_c, tile_rows, width = queries.shape
    head_count = log_norm.shape[3]
    head_width = width // head_count
    score_scale = head_width ** -0.5
    flat_count = tiles_f * tiles_r * tiles_c

    def split_heads(array_in):
        return array_in.astype(jnp.float32).reshape(array_in.shape[:-1] + (head_count, head_width))

    row_delta = jnp.sum(split_heads(cotangent) * split_heads(forward_out), axis=-1)
    log_rows = jnp.transpose(log_norm, (0, 1, 2, 4, 3))

    def padded(array_in):
        return jnp.pad(array_in, ((1, 1), (1, 1), (1, 1)) + ((0, 0),) * (array_in.ndim - 3))

    pad_q, pad_k, pad_v, pad_do = padded(queries), padded(key_vectors), padded(value_vectors), padded(cotangent)
    pad_log, pad_delta = padded(log_rows), padded(row_delta)
    flat_q = queries.reshape(flat_count, tile_rows, width)
    flat_k = key_vectors.reshape(flat_count, tile_rows, width)
    flat_v = value_vectors.reshape(flat_count, tile_rows, width)
    flat_do = cotangent.reshape(flat_count, tile_rows, width)
    flat_log = log_rows.reshape(flat_count, tile_rows, head_count)
    flat_delta = row_delta.reshape(flat_count, tile_rows, head_count)

    def one_tile(index):
        frame_at = index // (tiles_r * tiles_c)
        row_at = (index // tiles_c) % tiles_r
        col_at = index % tiles_c
        valid = jnp.repeat(window_valid(frame_at, row_at, col_at, tiles_f, tiles_r, tiles_c), tile_rows)
        own_q = split_heads(flat_q[index])
        own_k = split_heads(flat_k[index])
        own_v = split_heads(flat_v[index])
        own_do = split_heads(flat_do[index])
        own_log = flat_log[index]
        own_delta = flat_delta[index]
        near_q = split_heads(neighbours(pad_q, frame_at, row_at, col_at))
        near_k = split_heads(neighbours(pad_k, frame_at, row_at, col_at))
        near_v = split_heads(neighbours(pad_v, frame_at, row_at, col_at))
        near_do = split_heads(neighbours(pad_do, frame_at, row_at, col_at))
        near_log = neighbours(pad_log, frame_at, row_at, col_at)
        near_delta = neighbours(pad_delta, frame_at, row_at, col_at)

        scores = jnp.einsum('qhd,khd->hqk', own_q, near_k) * score_scale
        probs = jnp.where(valid[None, None, :], jnp.exp(scores - own_log.T[:, :, None]), 0.0)
        dprobs = jnp.einsum('qhd,khd->hqk', own_do, near_v)
        dscores = probs * (dprobs - own_delta.T[:, :, None])
        grad_q = jnp.einsum('hqk,khd->qhd', rounded(dscores), near_k) * score_scale

        scores_k = jnp.einsum('qhd,khd->hqk', near_q, own_k) * score_scale
        probs_k = jnp.where(valid[None, :, None], jnp.exp(scores_k - near_log.T[:, :, None]), 0.0)
        dprobs_k = jnp.einsum('qhd,khd->hqk', near_do, own_v)
        dscores_k = probs_k * (dprobs_k - near_delta.T[:, :, None])
        grad_v = jnp.einsum('hqk,qhd->khd', rounded(probs_k), near_do)
        grad_k = jnp.einsum('hqk,qhd->khd', rounded(dscores_k), near_q) * score_scale
        return (grad_q.reshape(tile_rows, width).astype(jnp.bfloat16),
                grad_k.reshape(tile_rows, width).astype(jnp.bfloat16),
                grad_v.reshape(tile_rows, width).astype(jnp.bfloat16))

    grads_q, grads_k, grads_v = lax.map(one_tile, jnp.arange(flat_count, dtype=jnp.int32))
    full_shape = (tiles_f, tiles_r, tiles_c, tile_rows, width)
    return grads_q.reshape(full_shape), grads_k.reshape(full_shape), grads_v.reshape(full_shape)
```

```python
import functools

import jax
import jax.numpy as jnp
from jax import lax
from jax.experimental import pallas as pl
from jax.experimental.pallas import tpu as pltpu
from jax.sharding import PartitionSpec as P

MESH = pl.DeviceIdType.MESH
LOG2E = 1.4426950408889634


def passed_along(x, axis, by):
    peers = lax.axis_size(axis)
    pairs = [(i, i + by) for i in range(peers) if 0 <= i + by < peers]
    return lax.ppermute(x, axis, pairs)


def with_halo(x, sides, width):
    for axis, dim in sides:
        peers, length = (lax.axis_size(axis), x.shape[dim])
        up = [(i, (i + 1) % peers) for i in range(peers - 1)]
        down = [(j, i) for i, j in up]
        last = lax.slice_in_dim(x, length - width, length, axis=dim)
        leading = lax.slice_in_dim(x, 0, width, axis=dim)
        before = lax.ppermute(last, axis, up)
        after = lax.ppermute(leading, axis, down)
        x = jnp.concatenate([before, x, after], axis=dim)
    return x


def window_valid():
    offsets = jnp.arange(3, dtype=jnp.int32) - 1
    frame_pos = lax.axis_index("frame") + offsets
    row_pos = lax.axis_index("row") + offsets
    col_pos = lax.axis_index("col") + offsets
    along_f = (frame_pos >= 0) & (frame_pos < lax.axis_size("frame"))
    along_r = (row_pos >= 0) & (row_pos < lax.axis_size("row"))
    along_c = (col_pos >= 0) & (col_pos < lax.axis_size("col"))
    return along_f[:, None, None] & along_r[None, :, None] & along_c[None, None, :]


def reduce_frame(partial_sums, dim):
    from_next = passed_along(lax.index_in_dim(partial_sums, 0, dim, keepdims=False), "frame", -1)
    from_prev = passed_along(lax.index_in_dim(partial_sums, 2, dim, keepdims=False), "frame", 1)
    return lax.index_in_dim(partial_sums, 1, dim, keepdims=False) + from_next + from_prev


def reduce_row(partial_sums, dim):
    from_next = passed_along(lax.index_in_dim(partial_sums, 0, dim, keepdims=False), "row", -1)
    from_prev = passed_along(lax.index_in_dim(partial_sums, 2, dim, keepdims=False), "row", 1)
    return lax.index_in_dim(partial_sums, 1, dim, keepdims=False) + from_next + from_prev


def reduce_col(partial_sums, dim):
    from_next = passed_along(lax.index_in_dim(partial_sums, 0, dim, keepdims=False), "col", -1)
    from_prev = passed_along(lax.index_in_dim(partial_sums, 2, dim, keepdims=False), "col", 1)
    return lax.index_in_dim(partial_sums, 1, dim, keepdims=False) + from_next + from_prev


def fold_back(partial_sums):
    partial_sums = reduce_frame(partial_sums, 0)
    partial_sums = reduce_row(partial_sums, 0)
    return reduce_col(partial_sums, 0)


def local(queries, key_vectors, value_vectors, forward_out, cotangent, log_norm):
    tile_rows = queries.shape[3]
    width = queries.shape[4]
    head_count = log_norm.shape[3]
    head_width = width // head_count
    score_scale = head_width ** (-0.5)
    valid = window_valid().reshape(9, 3)
    own_q = queries.reshape(tile_rows, head_count, head_width)
    own_do = cotangent.reshape(tile_rows, head_count, head_width)
    products = cotangent.astype(jnp.float32) * forward_out.astype(jnp.float32)
    row_delta = jnp.sum(products.reshape(tile_rows, head_count, head_width), axis=-1).T
    own_log = log_norm.reshape(head_count, tile_rows)
    out_shape = (1, 1, 1, tile_rows, width)
    joined = jnp.concatenate((key_vectors, value_vectors), axis=3)
    nearby = with_halo(joined, (("frame", 0), ("row", 1), ("col", 2)), 1)
    nearby = nearby.reshape(9, 3, 2 * tile_rows, width)

    def slab_step(grad_q, inputs):
        slab, valid_slab = inputs
        near_k = slab[:, :tile_rows].reshape(3 * tile_rows, head_count, head_width)
        near_v = slab[:, tile_rows:].reshape(3 * tile_rows, head_count, head_width)
        keep = jnp.repeat(valid_slab, tile_rows)
        scores = (
            jnp.einsum("qhd,khd->hqk", own_q, near_k, preferred_element_type=jnp.float32)
            * score_scale
        )
        probs = jnp.where(keep[None, None, :], jnp.exp(scores - own_log[:, :, None]), 0.0)
        dprobs = jnp.einsum("qhd,khd->hqk", own_do, near_v, preferred_element_type=jnp.float32)
        dscores = (probs * (dprobs - row_delta[:, :, None])).astype(jnp.bfloat16)
        grad_q = grad_q + jnp.einsum(
            "hqk,khd->qhd", dscores, near_k, preferred_element_type=jnp.float32
        )
        grad_k = jnp.einsum("hqk,qhd->khd", dscores, own_q, preferred_element_type=jnp.float32)
        grad_v = jnp.einsum(
            "hqk,qhd->khd", probs.astype(jnp.bfloat16), own_do, preferred_element_type=jnp.float32
        )
        stacked = jnp.concatenate(
            (grad_k.reshape(3, tile_rows, width), grad_v.reshape(3, tile_rows, width)), axis=1
        )
        return (grad_q, stacked)

    zeros = jnp.zeros((tile_rows, head_count, head_width), jnp.float32)
    grad_q, partial_sums = lax.scan(slab_step, zeros, (nearby, valid))
    folded = fold_back(partial_sums.reshape(3, 3, 3, 2 * tile_rows, width))
    grad_queries = grad_q.reshape(tile_rows, width) * score_scale
    grad_keys = folded[:tile_rows] * score_scale
    grad_values = folded[tile_rows:]
    return (
        grad_queries.astype(jnp.bfloat16).reshape(out_shape),
        grad_keys.astype(jnp.bfloat16).reshape(out_shape),
        grad_values.astype(jnp.bfloat16).reshape(out_shape),
    )


def arrived(ref, sem):
    pltpu.make_async_copy(ref, ref, sem).wait()


def window_kernel(
    rows,
    q_ref, k_ref, v_ref, o_ref, do_ref, log_ref,
    dq_ref, dk_ref, dv_ref,
    kv, qd, stat, stat_own, grads_out, grads_in, own_sum, partial, dq_sum, dq_in, final_kv, final_q,
    kv_send, kv_recv, q_send, q_recv, pass_send, halo_send, halo_recv,
    ret_send, ret_recv, dq_send, dq_recv, out_send, out_recv,
):
    f, r, b = lax.axis_index("frame"), lax.axis_index("row"), lax.axis_index("col")
    y, a = f // 2, f % 2
    tokens, width = q_ref.shape
    feats = width // 2
    scale = feats ** (-0.5)
    other_f = 2 * y + 1 - a
    across_f = f + 2 - 4 * y
    near = 1 - y
    has_row = {-1: r > 0, 1: r < rows - 1}

    barrier = pltpu.get_barrier_semaphore()

    def greet(where):
        pl.semaphore_signal(barrier, inc=1, device_id=where, device_id_type=MESH)

    for where in ((other_f, r, b), (f, r, 1 - b), (other_f, r, 1 - b), (across_f, r, b)):
        greet(where)
    for step in (-1, 1):
        @pl.when(has_row[step])
        def _():
            greet((f, r + step, b))
            greet((across_f, r + step, b))

    def cols(head):
        return pl.ds(pl.multiple_of(head * feats, feats), feats)

    def toks(col):
        return pl.ds(pl.multiple_of(col * tokens, 128), tokens)

    ones = jnp.ones((8, feats), jnp.bfloat16)
    along = (((1,), (1,)), ((), ()))
    for head in range(2):
        part = slice(head * feats, (head + 1) * feats)
        product = do_ref[:, part].astype(jnp.float32) * o_ref[:, part].astype(jnp.float32)
        high = product.astype(jnp.bfloat16)
        low = (product - high.astype(jnp.float32)).astype(jnp.bfloat16)
        delta = lax.dot_general(ones, high, along, preferred_element_type=jnp.float32)
        delta += lax.dot_general(ones, low, along, preferred_element_type=jnp.float32)
        stat_own[head] = delta
        stat_own[head, 0:1, :] = log_ref[head : head + 1, :] * LOG2E
    dq_sum[...] = jnp.zeros_like(dq_sum)

    pl.semaphore_wait(
        barrier, 4 + 2 * (has_row[-1].astype(jnp.int32) + has_row[1].astype(jnp.int32))
    )

    def remote(src, dst, send, recv, where):
        return pltpu.make_async_remote_copy(
            src_ref=src, dst_ref=dst, send_sem=send, recv_sem=recv, device_id=where, device_id_type=MESH
        )

    key_f = 2 * y + b
    stays = a == b
    for kind, ref in enumerate((k_ref, v_ref)):
        remote(
            ref.at[:, cols(1 - b)], kv.at[1, a, kind], kv_send.at[0, kind], kv_recv.at[a, kind],
            (key_f, r, 1 - b),
        ).start()
    for kind, ref in enumerate((k_ref, v_ref)):
        src, dst = ref.at[:, cols(b)], kv.at[1, a, kind]

        @pl.when(stays)
        def _():
            pltpu.make_async_copy(src, dst, kv_recv.at[a, kind]).start()

        @pl.when(jnp.logical_not(stays))
        def _():
            remote(src, dst, kv_send.at[1, kind], kv_recv.at[a, kind], (key_f, r, b)).start()

    def q_slot(kind, frame, col):
        if kind == 2:
            return stat.at[frame, :, toks(col)]
        return qd.at[frame, kind, toks(col)]

    def q_source(kind, head):
        if kind == 2:
            return stat_own.at[head]
        return (q_ref, do_ref)[kind].at[:, cols(head)]

    for kind in range(3):
        remote(
            q_source(kind, 1 - b), q_slot(kind, a, b), q_send.at[0, kind], q_recv.at[a, b, kind],
            (f, r, 1 - b),
        ).start()
    for kind in range(3):
        remote(
            q_source(kind, b), q_slot(kind, a, b), q_send.at[1, kind], q_recv.at[a, b, kind],
            (other_f, r, b),
        ).start()
        pltpu.make_async_copy(q_source(kind, b), q_slot(kind, a, b), q_recv.at[a, b, kind]).start()

    for frame in range(2):
        for kind in range(2):
            arrived(kv.at[1, frame, kind], kv_recv.at[frame, kind])
        for step in (-1, 1):
            @pl.when(has_row[step])
            def _():
                remote(
                    kv.at[1, frame], kv.at[1 - step, frame], halo_send.at[1 - step, frame],
                    halo_recv.at[1 - step, frame], (f, r + step, b),
                ).start()

        @pl.when(near == frame)
        def _():
            remote(
                kv.at[1, frame], kv.at[1, 2], halo_send.at[1, 2], halo_recv.at[1, 2], (across_f, r, b)
            ).start()
            for step in (-1, 1):
                @pl.when(has_row[step])
                def _():
                    remote(
                        kv.at[1, frame], kv.at[1 - step, 2], halo_send.at[1 - step, 2],
                        halo_recv.at[1 - step, 2], (across_f, r + step, b),
                    ).start()

    for kind in range(3):
        arrived(q_slot(kind, a, 1 - b), q_recv.at[a, 1 - b, kind])
        remote(
            q_slot(kind, a, 1 - b), q_slot(kind, a, 1 - b), pass_send.at[kind],
            q_recv.at[a, 1 - b, kind], (other_f, r, b),
        ).start()
    for frame, col in ((a, b), (1 - a, b), (1 - a, 1 - b)):
        for kind in range(3):
            arrived(q_slot(kind, frame, col), q_recv.at[frame, col, kind])

    chunk = 256
    count = 2 * tokens // chunk

    def one_frame(at_row, at_frame, frame):
        keys = kv[at_row, at_frame, 0]
        values = kv[at_row, at_frame, 1]

        def products(at):
            some = slice(at * chunk, (at + 1) * chunk)
            q_part = qd[frame, 0, some, :]
            do_part = qd[frame, 1, some, :]
            scores = lax.dot_general(keys, q_part, along, preferred_element_type=jnp.float32)
            dprobs = lax.dot_general(values, do_part, along, preferred_element_type=jnp.float32)
            return q_part, do_part, scores, dprobs

        dk = dv = None
        upcoming = products(0)
        for at in range(count):
            some = slice(at * chunk, (at + 1) * chunk)
            q_part, do_part, scores, dprobs = upcoming
            if at + 1 < count:
                upcoming = products(at + 1)
            probs = jnp.exp2(scores * (scale * LOG2E) - stat[frame, 0:1, some])
            dscores = probs * (dprobs - stat[frame, 1:2, some])
            probs = probs.astype(jnp.bfloat16)
            dscores = dscores.astype(jnp.bfloat16)
            dv_part = jnp.dot(probs, do_part, preferred_element_type=jnp.float32)
            dk_part = jnp.dot(dscores, q_part, preferred_element_type=jnp.float32)
            dv = dv_part if dv is None else dv + dv_part
            dk = dk_part if dk is None else dk + dk_part
            dq_sum[frame, some, :] += lax.dot_general(
                dscores, keys, (((0,), (0,)), ((), ())), preferred_element_type=jnp.float32
            )
        partial[0] += dk
        partial[1] += dv

    def one_tile(at, carry):
        at_row, at_frame = (at // 3 + 1) % 3, at % 3
        to_row = r + at_row - 1
        outer = at_frame // 2

        @pl.when((to_row >= 0) & (to_row < rows))
        def _():
            @pl.when(at >= 2)
            def _():
                arrived(kv.at[at_row, at_frame], halo_recv.at[at_row, at_frame])

            partial[...] = jnp.zeros_like(partial)

            def over_frames(step, carry):
                one_frame(at_row, at_frame, step + near * outer)
                return carry

            lax.fori_loop(0, 2 - outer, over_frames, 0)

            @pl.when(at < 2)
            def _():
                own_sum[at_frame] = partial[...]

            @pl.when(at >= 2)
            def _():
                grads_out[at_row, at_frame] = partial[...].astype(jnp.bfloat16)
                remote(
                    grads_out.at[at_row, at_frame], grads_in.at[2 - at_row, at_frame],
                    ret_send.at[at_row, at_frame], ret_recv.at[2 - at_row, at_frame],
                    (f + outer * (2 - 4 * y), to_row, b),
                ).start()

        return carry

    lax.fori_loop(0, 9, one_tile, 0)

    dq_copy = remote(dq_sum.at[1 - a], dq_in, dq_send, dq_recv, (other_f, r, b))
    dq_copy.start()
    dq_copy.wait_recv()
    final_q[...] = ((dq_sum[a] + dq_in[...]) * scale).astype(jnp.bfloat16)
    mine = pltpu.make_async_copy(final_q.at[toks(b)], dq_ref.at[:, cols(b)], out_recv.at[0, b])
    mine.start()
    remote(
        final_q.at[toks(1 - b)], dq_ref.at[:, cols(b)], out_send.at[2, 0], out_recv.at[0, b], (f, r, 1 - b)
    ).start()

    for frame in range(2):
        for step in (-1, 1):
            @pl.when(has_row[step])
            def _():
                arrived(grads_in.at[1 + step, frame], ret_recv.at[1 + step, frame])
                own_sum[frame] += grads_in[1 + step, frame].astype(jnp.float32)

        @pl.when(near == frame)
        def _():
            arrived(grads_in.at[1, 2], ret_recv.at[1, 2])
            own_sum[frame] += grads_in[1, 2].astype(jnp.float32)
            for step in (-1, 1):
                @pl.when(has_row[step])
                def _():
                    arrived(grads_in.at[1 + step, 2], ret_recv.at[1 + step, 2])
                    own_sum[frame] += grads_in[1 + step, 2].astype(jnp.float32)

        final_kv[frame, 0] = (own_sum[frame, 0] * scale).astype(jnp.bfloat16)
        final_kv[frame, 1] = own_sum[frame, 1].astype(jnp.bfloat16)
        stays_here = (a == frame) & (a == b)
        for kind, ref in enumerate((dk_ref, dv_ref)):
            src, dst = final_kv.at[frame, kind], ref.at[:, cols(b)]

            @pl.when(stays_here)
            def _():
                pltpu.make_async_copy(src, dst, out_recv.at[1 + kind, b]).start()

            @pl.when(jnp.logical_not(stays_here))
            def _():
                remote(
                    src, dst, out_send.at[frame, kind], out_recv.at[1 + kind, b], (2 * y + frame, r, a)
                ).start()

    for kind in range(3):
        out = (dq_ref, dk_ref, dv_ref)[kind]
        for head in range(2):
            arrived(out.at[:, head * feats : (head + 1) * feats], out_recv.at[kind, head])
    dq_copy.wait_send()
    arrived(final_q.at[toks(1 - b)], out_send.at[2, 0])
    for kind in range(2):
        arrived(kv.at[1, 0, kind], kv_send.at[0, kind])

        @pl.when(jnp.logical_not(stays))
        def _():
            arrived(kv.at[1, 0, kind], kv_send.at[1, kind])

        for frame in range(2):
            @pl.when(jnp.logical_not((a == frame) & (a == b)))
            def _():
                arrived(final_kv.at[frame, kind], out_send.at[frame, kind])

    for kind in range(3):
        for which in range(2):
            arrived(q_source(kind, 0), q_send.at[which, kind])
        arrived(q_source(kind, 0), pass_send.at[kind])
    arrived(kv.at[1, 2], halo_send.at[1, 2])
    arrived(grads_out.at[1, 2], ret_send.at[1, 2])
    for step in (-1, 1):
        @pl.when(has_row[step])
        def _():
            for frame in range(3):
                arrived(kv.at[1 - step, frame], halo_send.at[1 - step, frame])
                arrived(grads_out.at[1 + step, frame], ret_send.at[1 + step, frame])


def local_window(rows, queries, key_vectors, value_vectors, forward_out, cotangent, log_norm):
    shape = queries.shape
    tokens, width = shape[3:]
    feats = width // 2
    flat = [x.reshape(tokens, width) for x in (queries, key_vectors, value_vectors, forward_out, cotangent)]
    half = (tokens, feats)
    low, full = jnp.bfloat16, jnp.float32
    dma = pltpu.SemaphoreType.DMA
    any_space = pl.BlockSpec(memory_space=pl.ANY)
    vmem = pl.BlockSpec(memory_space=pltpu.VMEM)
    outs = pl.pallas_call(
        functools.partial(window_kernel, rows),
        out_shape=[jax.ShapeDtypeStruct((tokens, width), low)] * 3,
        in_specs=[any_space, any_space, any_space, vmem, vmem, vmem],
        out_specs=[any_space] * 3,
        scratch_shapes=[
            pltpu.VMEM((3, 3, 2) + half, low),
            pltpu.VMEM((2, 2, 2 * tokens, feats), low),
            pltpu.VMEM((2, 8, 2 * tokens), full),
            pltpu.VMEM((2, 8, tokens), full),
            pltpu.VMEM((3, 3, 2) + half, low),
            pltpu.VMEM((3, 3, 2) + half, low),
            pltpu.VMEM((2, 2) + half, full),
            pltpu.VMEM((2,) + half, full),
            pltpu.VMEM((2, 2 * tokens, feats), full),
            pltpu.VMEM((2 * tokens, feats), full),
            pltpu.VMEM((2, 2) + half, low),
            pltpu.VMEM((2 * tokens, feats), low),
            dma((2, 2)), dma((2, 2)), dma((2, 3)), dma((2, 2, 3)), dma((3,)), dma((3, 3)), dma((3, 3)),
            dma((3, 3)), dma((3, 3)), dma, dma, dma((3, 2)), dma((3, 2)),
        ],
        compiler_params=pltpu.CompilerParams(
            collective_id=0, has_side_effects=True, vmem_limit_bytes=40 * 2**20
        ),
    )(*flat, log_norm.reshape(2, tokens))
    return tuple(x.reshape(shape) for x in outs)


def solution(mesh):
    placed = (P("frame", "row", "col", None, None),) * 6
    sizes = dict(mesh.shape)
    body = local
    if sizes["frame"] == 4 and sizes["col"] == 2:
        body = functools.partial(local_window, sizes["row"])
    return jax.shard_map(
        body,
        mesh=mesh,
        in_specs=placed,
        out_specs=placed[:3],
        check_vma=False,
    )
```

```python
import functools

import jax
import jax.numpy as jnp
from jax import lax
from jax.experimental import pallas as pl
from jax.experimental.pallas import tpu as pltpu
from jax.sharding import PartitionSpec as P

MESH = pl.DeviceIdType.MESH
LOG2E = 1.4426950408889634


def passed_along(x, axis, by):
    peers = lax.axis_size(axis)
    pairs = [(i, i + by) for i in range(peers) if 0 <= i + by < peers]
    return lax.ppermute(x, axis, pairs)


def with_halo(x, sides, width):
    for axis, dim in sides:
        peers, length = (lax.axis_size(axis), x.shape[dim])
        up = [(i, (i + 1) % peers) for i in range(peers - 1)]
        down = [(j, i) for i, j in up]
        last = lax.slice_in_dim(x, length - width, length, axis=dim)
        leading = lax.slice_in_dim(x, 0, width, axis=dim)
        before = lax.ppermute(last, axis, up)
        after = lax.ppermute(leading, axis, down)
        x = jnp.concatenate([before, x, after], axis=dim)
    return x


def window_valid():
    offsets = jnp.arange(3, dtype=jnp.int32) - 1
    frame_pos = lax.axis_index("frame") + offsets
    row_pos = lax.axis_index("row") + offsets
    col_pos = lax.axis_index("col") + offsets
    along_f = (frame_pos >= 0) & (frame_pos < lax.axis_size("frame"))
    along_r = (row_pos >= 0) & (row_pos < lax.axis_size("row"))
    along_c = (col_pos >= 0) & (col_pos < lax.axis_size("col"))
    return along_f[:, None, None] & along_r[None, :, None] & along_c[None, None, :]


def reduce_frame(partial_sums, dim):
    from_next = passed_along(lax.index_in_dim(partial_sums, 0, dim, keepdims=False), "frame", -1)
    from_prev = passed_along(lax.index_in_dim(partial_sums, 2, dim, keepdims=False), "frame", 1)
    return lax.index_in_dim(partial_sums, 1, dim, keepdims=False) + from_next + from_prev


def reduce_row(partial_sums, dim):
    from_next = passed_along(lax.index_in_dim(partial_sums, 0, dim, keepdims=False), "row", -1)
    from_prev = passed_along(lax.index_in_dim(partial_sums, 2, dim, keepdims=False), "row", 1)
    return lax.index_in_dim(partial_sums, 1, dim, keepdims=False) + from_next + from_prev


def reduce_col(partial_sums, dim):
    from_next = passed_along(lax.index_in_dim(partial_sums, 0, dim, keepdims=False), "col", -1)
    from_prev = passed_along(lax.index_in_dim(partial_sums, 2, dim, keepdims=False), "col", 1)
    return lax.index_in_dim(partial_sums, 1, dim, keepdims=False) + from_next + from_prev


def fold_back(partial_sums):
    partial_sums = reduce_frame(partial_sums, 0)
    partial_sums = reduce_row(partial_sums, 0)
    return reduce_col(partial_sums, 0)


def local(queries, key_vectors, value_vectors, forward_out, cotangent, log_norm):
    tile_rows = queries.shape[3]
    width = queries.shape[4]
    head_count = log_norm.shape[3]
    head_width = width // head_count
    score_scale = head_width ** (-0.5)
    valid = window_valid().reshape(9, 3)
    own_q = queries.reshape(tile_rows, head_count, head_width)
    own_do = cotangent.reshape(tile_rows, head_count, head_width)
    products = cotangent.astype(jnp.float32) * forward_out.astype(jnp.float32)
    row_delta = jnp.sum(products.reshape(tile_rows, head_count, head_width), axis=-1).T
    own_log = log_norm.reshape(head_count, tile_rows)
    out_shape = (1, 1, 1, tile_rows, width)
    joined = jnp.concatenate((key_vectors, value_vectors), axis=3)
    nearby = with_halo(joined, (("frame", 0), ("row", 1), ("col", 2)), 1)
    nearby = nearby.reshape(9, 3, 2 * tile_rows, width)

    def slab_step(grad_q, inputs):
        slab, valid_slab = inputs
        near_k = slab[:, :tile_rows].reshape(3 * tile_rows, head_count, head_width)
        near_v = slab[:, tile_rows:].reshape(3 * tile_rows, head_count, head_width)
        keep = jnp.repeat(valid_slab, tile_rows)
        scores = (
            jnp.einsum("qhd,khd->hqk", own_q, near_k, preferred_element_type=jnp.float32)
            * score_scale
        )
        probs = jnp.where(keep[None, None, :], jnp.exp(scores - own_log[:, :, None]), 0.0)
        dprobs = jnp.einsum("qhd,khd->hqk", own_do, near_v, preferred_element_type=jnp.float32)
        dscores = (probs * (dprobs - row_delta[:, :, None])).astype(jnp.bfloat16)
        grad_q = grad_q + jnp.einsum(
            "hqk,khd->qhd", dscores, near_k, preferred_element_type=jnp.float32
        )
        grad_k = jnp.einsum("hqk,qhd->khd", dscores, own_q, preferred_element_type=jnp.float32)
        grad_v = jnp.einsum(
            "hqk,qhd->khd", probs.astype(jnp.bfloat16), own_do, preferred_element_type=jnp.float32
        )
        stacked = jnp.concatenate(
            (grad_k.reshape(3, tile_rows, width), grad_v.reshape(3, tile_rows, width)), axis=1
        )
        return (grad_q, stacked)

    zeros = jnp.zeros((tile_rows, head_count, head_width), jnp.float32)
    grad_q, partial_sums = lax.scan(slab_step, zeros, (nearby, valid))
    folded = fold_back(partial_sums.reshape(3, 3, 3, 2 * tile_rows, width))
    grad_queries = grad_q.reshape(tile_rows, width) * score_scale
    grad_keys = folded[:tile_rows] * score_scale
    grad_values = folded[tile_rows:]
    return (
        grad_queries.astype(jnp.bfloat16).reshape(out_shape),
        grad_keys.astype(jnp.bfloat16).reshape(out_shape),
        grad_values.astype(jnp.bfloat16).reshape(out_shape),
    )


def arrived(ref, sem):
    pltpu.make_async_copy(ref, ref, sem).wait()


def window_kernel(
    rows,
    q_ref, k_ref, v_ref, o_ref, do_ref, log_ref,
    dq_ref, dk_ref, dv_ref,
    kv, qd, stat, stat_own, o_in, do_in, log_in, grads_out, grads_in, sums, dq_sum, dq_out, dq_in,
    final_kv, final_q,
    load_sem, kv_send, kv_recv, q_send, q_recv, halo_send, halo_recv,
    ret_send, ret_recv, dq_send, dq_recv, out_send, out_recv,
):
    f, r, b = lax.axis_index("frame"), lax.axis_index("row"), lax.axis_index("col")
    y, a = f // 2, f % 2
    tokens, width = q_ref.shape
    feats = width // 2
    scale = feats ** (-0.5)
    other_f = 2 * y + 1 - a
    across_f = f + 2 - 4 * y
    near = 1 - y
    has_row = {-1: r > 0, 1: r < rows - 1}

    barrier = pltpu.get_barrier_semaphore()

    def greet(where):
        pl.semaphore_signal(barrier, inc=1, device_id=where, device_id_type=MESH)

    for where in ((other_f, r, b), (f, r, 1 - b), (other_f, r, 1 - b), (across_f, r, b)):
        greet(where)
    for step in (-1, 1):
        @pl.when(has_row[step])
        def _():
            greet((f, r + step, b))
            greet((across_f, r + step, b))

    def cols(head):
        return pl.ds(pl.multiple_of(head * feats, feats), feats)

    def toks(frame):
        return pl.ds(pl.multiple_of(frame * tokens, 128), tokens)

    def remote(src, dst, send, recv, where):
        return pltpu.make_async_remote_copy(
            src_ref=src, dst_ref=dst, send_sem=send, recv_sem=recv, device_id=where, device_id_type=MESH
        )

    def q_slot(kind, frame, col):
        if kind == 2:
            return stat.at[col, :, toks(frame)]
        return qd.at[col, kind, toks(frame)]

    def q_source(kind, head):
        if kind == 2:
            return stat_own.at[head]
        return (q_ref, do_ref)[kind].at[:, cols(head)]

    def q_local(kind):
        pltpu.make_async_copy(q_source(kind, a), q_slot(kind, a, b), q_recv.at[b, a, kind]).start()

    def q_remote(kind, which):
        head, col = ((1 - a, b), (a, 1 - b), (1 - a, 1 - b))[which]
        remote(
            q_source(kind, head), q_slot(kind, a, b), q_send.at[which, kind], q_recv.at[b, a, kind],
            (2 * y + head, r, col),
        ).start()

    loads = [
        pltpu.make_async_copy(src, dst, load_sem.at[at])
        for at, (src, dst) in enumerate(((do_ref, do_in), (o_ref, o_in), (log_ref, log_in)))
    ]
    for kind, ref in enumerate((k_ref, v_ref)):
        pltpu.make_async_copy(ref.at[:, cols(a)], kv.at[1, a, kind], kv_recv.at[a, kind]).start()
    for load in loads:
        load.start()
    for kind in range(2):
        q_local(kind)

    pl.semaphore_wait(
        barrier, 4 + 2 * (has_row[-1].astype(jnp.int32) + has_row[1].astype(jnp.int32))
    )

    for kind, ref in enumerate((k_ref, v_ref)):
        remote(
            ref.at[:, cols(1 - a)], kv.at[1, a, kind], kv_send.at[kind], kv_recv.at[a, kind], (other_f, r, b)
        ).start()
    for which in range(3):
        for kind in range(2):
            q_remote(kind, which)

    for frame in (a, 1 - a):
        for kind in range(2):
            arrived(kv.at[1, frame, kind], kv_recv.at[frame, kind])
        for step in (-1, 1):
            @pl.when(has_row[step])
            def _():
                remote(
                    kv.at[1, frame], kv.at[1 - step, frame], halo_send.at[1 - step, frame],
                    halo_recv.at[1 - step, frame], (f, r + step, b),
                ).start()

        @pl.when(near == frame)
        def _():
            remote(
                kv.at[1, frame], kv.at[1, 2], halo_send.at[1, 2], halo_recv.at[1, 2], (across_f, r, b)
            ).start()
            for step in (-1, 1):
                @pl.when(has_row[step])
                def _():
                    remote(
                        kv.at[1, frame], kv.at[1 - step, 2], halo_send.at[1 - step, 2],
                        halo_recv.at[1 - step, 2], (across_f, r + step, b),
                    ).start()

    for load in loads:
        load.wait()
    ones = jnp.ones((8, feats), jnp.bfloat16)
    along = (((1,), (1,)), ((), ()))
    for head in range(2):
        part = slice(head * feats, (head + 1) * feats)
        product = do_in[:, part].astype(jnp.float32) * o_in[:, part].astype(jnp.float32)
        high = product.astype(jnp.bfloat16)
        low = (product - high.astype(jnp.float32)).astype(jnp.bfloat16)
        delta = lax.dot_general(ones, high, along, preferred_element_type=jnp.float32)
        delta += lax.dot_general(ones, low, along, preferred_element_type=jnp.float32)
        stat_own[head] = delta
        stat_own[head, 0:1, :] = log_in[head : head + 1, :] * LOG2E
    q_local(2)
    for which in range(3):
        q_remote(2, which)
    dq_sum[...] = jnp.zeros_like(dq_sum)

    def one_block(at_row, at_frame, col, first):
        keys = kv[at_row, at_frame, 0]
        values = kv[at_row, at_frame, 1]
        keys_t = keys.T
        if isinstance(at_frame, int) and at_frame == 2:
            chunks = [toks(near)]
        else:
            chunks = [pl.ds(at, 256) for at in range(0, 2 * tokens, 256)]

        def products(some):
            q_part = qd[col, 0, some, :]
            do_part = qd[col, 1, some, :]
            scores = lax.dot_general(keys, q_part, along, preferred_element_type=jnp.float32)
            dprobs = lax.dot_general(values, do_part, along, preferred_element_type=jnp.float32)
            return q_part, do_part, scores, dprobs

        dk = dv = None
        upcoming = products(chunks[0])
        for at, some in enumerate(chunks):
            q_part, do_part, scores, dprobs = upcoming
            if at + 1 < len(chunks):
                upcoming = products(chunks[at + 1])
            probs = jnp.exp2(scores * (scale * LOG2E) - stat[col, 0:1, some])
            dscores = probs * (dprobs - stat[col, 1:2, some])
            probs = probs.astype(jnp.bfloat16)
            dscores = dscores.astype(jnp.bfloat16)
            dv_part = jnp.dot(probs, do_part, preferred_element_type=jnp.float32)
            dk_part = jnp.dot(dscores, q_part, preferred_element_type=jnp.float32)
            dv = dv_part if dv is None else dv + dv_part
            dk = dk_part if dk is None else dk + dk_part
            dq_sum[col, :, some] += jnp.dot(keys_t, dscores, preferred_element_type=jnp.float32)
        if first:
            sums[at_row, at_frame, 0] = dk
            sums[at_row, at_frame, 1] = dv
        else:
            sums[at_row, at_frame, 0] += dk
            sums[at_row, at_frame, 1] += dv

    def give_back(at_row, at_frame):
        grads_out[at_row, at_frame] = sums[at_row, at_frame].astype(jnp.bfloat16)
        remote(
            grads_out.at[at_row, at_frame], grads_in.at[2 - at_row, at_frame],
            ret_send.at[at_row, at_frame], ret_recv.at[2 - at_row, at_frame],
            (across_f if at_frame == 2 else f, r + at_row - 1, b),
        ).start()

    def q_arrived(col):
        for frame in range(2):
            for kind in range(3):
                arrived(q_slot(kind, frame, col), q_recv.at[col, frame, kind])

    def own_row(col, first):
        def body(frame, carry):
            one_block(1, frame, col, first)
            return carry

        lax.fori_loop(0, 2, body, 0)

    def both_sides(frame, wait, blocks, back):
        def body(side, carry):
            at_row = 2 * side
            to_row = r + at_row - 1

            @pl.when((to_row >= 0) & (to_row < rows))
            def _():
                if wait:
                    arrived(kv.at[at_row, frame], halo_recv.at[at_row, frame])
                for col, first in blocks:
                    one_block(at_row, frame, col, first)
                if back:
                    give_back(at_row, frame)

            return carry

        lax.fori_loop(0, 2, body, 0)

    def send_dq(frame, which):
        dq_out[:, toks(frame)] = dq_sum[1 - b, :, toks(frame)].astype(jnp.bfloat16)
        remote(
            dq_out.at[:, toks(frame)], dq_in.at[:, toks(frame)], dq_send.at[which], dq_recv.at[which],
            (f, r, 1 - b),
        ).start()

    q_arrived(b)
    own_row(b, True)
    arrived(kv.at[1, 2], halo_recv.at[1, 2])
    one_block(1, 2, b, True)
    both_sides(0, True, ((b, True),), False)
    q_arrived(1 - b)
    both_sides(0, False, ((1 - b, False),), True)
    one_block(1, 2, 1 - b, False)
    give_back(1, 2)
    both_sides(1, True, ((b, True), (1 - b, False)), True)
    own_row(1 - b, False)
    send_dq(1 - near, 0)
    both_sides(2, True, ((1 - b, True), (b, False)), True)
    send_dq(near, 1)

    def add_back(frame, at_row, at_frame):
        arrived(grads_in.at[at_row, at_frame], ret_recv.at[at_row, at_frame])
        sums[1, frame] += grads_in[at_row, at_frame].astype(jnp.float32)

    def finish_keys(frame):
        for step in (-1, 1):
            @pl.when(has_row[step])
            def _():
                add_back(frame, 1 + step, frame)

    def hand_out(kind, frame, src, ref):
        dst = ref.at[:, cols(a)]

        @pl.when(frame == a)
        def _():
            pltpu.make_async_copy(src, dst, out_recv.at[kind, a]).start()

        @pl.when(frame != a)
        def _():
            remote(src, dst, out_send.at[kind], out_recv.at[kind, a], (other_f, r, b)).start()

    def hand_out_keys(frame):
        final_kv[frame, 0] = (sums[1, frame, 0] * scale).astype(jnp.bfloat16)
        final_kv[frame, 1] = sums[1, frame, 1].astype(jnp.bfloat16)
        for kind, ref in ((1, dk_ref), (2, dv_ref)):
            hand_out(kind, frame, final_kv.at[frame, kind - 1], ref)

    def hand_out_queries(frame, which):
        arrived(dq_in.at[:, toks(frame)], dq_recv.at[which])
        total = dq_sum[b, :, toks(frame)] + dq_in[:, toks(frame)].astype(jnp.float32)
        final_q[toks(frame), :] = (total * scale).T.astype(jnp.bfloat16)
        hand_out(0, frame, final_q.at[toks(frame)], dq_ref)

    finish_keys(1 - near)
    hand_out_keys(1 - near)
    hand_out_queries(1 - near, 0)
    finish_keys(near)
    add_back(near, 1, 2)
    hand_out_queries(near, 1)
    for step in (-1, 1):
        @pl.when(has_row[step])
        def _():
            add_back(near, 1 + step, 2)
    hand_out_keys(near)

    for kind in range(3):
        out = (dq_ref, dk_ref, dv_ref)[kind]
        for head in range(2):
            arrived(out.at[:, head * feats : (head + 1) * feats], out_recv.at[kind, head])
        arrived(final_kv.at[0, 0], out_send.at[kind])
        for which in range(3):
            arrived(q_source(kind, 0), q_send.at[which, kind])
    for which in range(2):
        arrived(kv.at[1, 0, which], kv_send.at[which])
        arrived(dq_out.at[:, toks(0)], dq_send.at[which])
    arrived(kv.at[1, 2], halo_send.at[1, 2])
    arrived(grads_out.at[1, 2], ret_send.at[1, 2])
    for step in (-1, 1):
        @pl.when(has_row[step])
        def _():
            for frame in range(3):
                arrived(kv.at[1 - step, frame], halo_send.at[1 - step, frame])
                arrived(grads_out.at[1 + step, frame], ret_send.at[1 + step, frame])


def local_window(rows, queries, key_vectors, value_vectors, forward_out, cotangent, log_norm):
    shape = queries.shape
    tokens, width = shape[3:]
    feats = width // 2
    flat = [x.reshape(tokens, width) for x in (queries, key_vectors, value_vectors, forward_out, cotangent)]
    half = (tokens, feats)
    low, full = jnp.bfloat16, jnp.float32
    dma = pltpu.SemaphoreType.DMA
    any_space = pl.BlockSpec(memory_space=pl.ANY)
    outs = pl.pallas_call(
        functools.partial(window_kernel, rows),
        out_shape=[jax.ShapeDtypeStruct((tokens, width), low)] * 3,
        in_specs=[any_space] * 6,
        out_specs=[any_space] * 3,
        scratch_shapes=[
            pltpu.VMEM((3, 3, 2) + half, low),
            pltpu.VMEM((2, 2, 2 * tokens, feats), low),
            pltpu.VMEM((2, 8, 2 * tokens), full),
            pltpu.VMEM((2, 8, tokens), full),
            pltpu.VMEM((tokens, width), low),
            pltpu.VMEM((tokens, width), low),
            pltpu.VMEM((2, tokens), full),
            pltpu.VMEM((3, 3, 2) + half, low),
            pltpu.VMEM((3, 3, 2) + half, low),
            pltpu.VMEM((3, 3, 2) + half, full),
            pltpu.VMEM((2, feats, 2 * tokens), full),
            pltpu.VMEM((feats, 2 * tokens), low),
            pltpu.VMEM((feats, 2 * tokens), low),
            pltpu.VMEM((2, 2) + half, low),
            pltpu.VMEM((2 * tokens, feats), low),
            dma((3,)), dma((2,)), dma((2, 2)), dma((3, 3)), dma((2, 2, 3)), dma((3, 3)), dma((3, 3)),
            dma((3, 3)), dma((3, 3)), dma((2,)), dma((2,)), dma((3,)), dma((3, 2)),
        ],
        compiler_params=pltpu.CompilerParams(
            collective_id=0, has_side_effects=True, vmem_limit_bytes=60 * 2**20
        ),
    )(*flat, log_norm.reshape(2, tokens))
    return tuple(x.reshape(shape) for x in outs)


def solution(mesh):
    placed = (P("frame", "row", "col", None, None),) * 6
    sizes = dict(mesh.shape)
    body = local
    if sizes["frame"] == 4 and sizes["col"] == 2:
        body = functools.partial(local_window, sizes["row"])
    return jax.shard_map(
        body,
        mesh=mesh,
        in_specs=placed,
        out_specs=placed[:3],
        check_vma=False,
    )
```

```python
import functools

import jax
import jax.numpy as jnp
from jax import lax
from jax.experimental import pallas as pl
from jax.experimental.pallas import tpu as pltpu
from jax.sharding import PartitionSpec as P

MESH = pl.DeviceIdType.MESH
LOG2E = 1.4426950408889634


def passed_along(x, axis, by):
    peers = lax.axis_size(axis)
    pairs = [(i, i + by) for i in range(peers) if 0 <= i + by < peers]
    return lax.ppermute(x, axis, pairs)


def with_halo(x, sides, width):
    for axis, dim in sides:
        peers, length = (lax.axis_size(axis), x.shape[dim])
        up = [(i, (i + 1) % peers) for i in range(peers - 1)]
        down = [(j, i) for i, j in up]
        last = lax.slice_in_dim(x, length - width, length, axis=dim)
        leading = lax.slice_in_dim(x, 0, width, axis=dim)
        before = lax.ppermute(last, axis, up)
        after = lax.ppermute(leading, axis, down)
        x = jnp.concatenate([before, x, after], axis=dim)
    return x


def window_valid():
    offsets = jnp.arange(3, dtype=jnp.int32) - 1
    frame_pos = lax.axis_index("frame") + offsets
    row_pos = lax.axis_index("row") + offsets
    col_pos = lax.axis_index("col") + offsets
    along_f = (frame_pos >= 0) & (frame_pos < lax.axis_size("frame"))
    along_r = (row_pos >= 0) & (row_pos < lax.axis_size("row"))
    along_c = (col_pos >= 0) & (col_pos < lax.axis_size("col"))
    return along_f[:, None, None] & along_r[None, :, None] & along_c[None, None, :]


def reduce_frame(partial_sums, dim):
    from_next = passed_along(lax.index_in_dim(partial_sums, 0, dim, keepdims=False), "frame", -1)
    from_prev = passed_along(lax.index_in_dim(partial_sums, 2, dim, keepdims=False), "frame", 1)
    return lax.index_in_dim(partial_sums, 1, dim, keepdims=False) + from_next + from_prev


def reduce_row(partial_sums, dim):
    from_next = passed_along(lax.index_in_dim(partial_sums, 0, dim, keepdims=False), "row", -1)
    from_prev = passed_along(lax.index_in_dim(partial_sums, 2, dim, keepdims=False), "row", 1)
    return lax.index_in_dim(partial_sums, 1, dim, keepdims=False) + from_next + from_prev


def reduce_col(partial_sums, dim):
    from_next = passed_along(lax.index_in_dim(partial_sums, 0, dim, keepdims=False), "col", -1)
    from_prev = passed_along(lax.index_in_dim(partial_sums, 2, dim, keepdims=False), "col", 1)
    return lax.index_in_dim(partial_sums, 1, dim, keepdims=False) + from_next + from_prev


def fold_back(partial_sums):
    partial_sums = reduce_frame(partial_sums, 0)
    partial_sums = reduce_row(partial_sums, 0)
    return reduce_col(partial_sums, 0)


def local(queries, key_vectors, value_vectors, forward_out, cotangent, log_norm):
    tile_rows = queries.shape[3]
    width = queries.shape[4]
    head_count = log_norm.shape[3]
    head_width = width // head_count
    score_scale = head_width ** (-0.5)
    valid = window_valid().reshape(9, 3)
    own_q = queries.reshape(tile_rows, head_count, head_width)
    own_do = cotangent.reshape(tile_rows, head_count, head_width)
    products = cotangent.astype(jnp.float32) * forward_out.astype(jnp.float32)
    row_delta = jnp.sum(products.reshape(tile_rows, head_count, head_width), axis=-1).T
    own_log = log_norm.reshape(head_count, tile_rows)
    out_shape = (1, 1, 1, tile_rows, width)
    joined = jnp.concatenate((key_vectors, value_vectors), axis=3)
    nearby = with_halo(joined, (("frame", 0), ("row", 1), ("col", 2)), 1)
    nearby = nearby.reshape(9, 3, 2 * tile_rows, width)

    def slab_step(grad_q, inputs):
        slab, valid_slab = inputs
        near_k = slab[:, :tile_rows].reshape(3 * tile_rows, head_count, head_width)
        near_v = slab[:, tile_rows:].reshape(3 * tile_rows, head_count, head_width)
        keep = jnp.repeat(valid_slab, tile_rows)
        scores = (
            jnp.einsum("qhd,khd->hqk", own_q, near_k, preferred_element_type=jnp.float32)
            * score_scale
        )
        probs = jnp.where(keep[None, None, :], jnp.exp(scores - own_log[:, :, None]), 0.0)
        dprobs = jnp.einsum("qhd,khd->hqk", own_do, near_v, preferred_element_type=jnp.float32)
        dscores = (probs * (dprobs - row_delta[:, :, None])).astype(jnp.bfloat16)
        grad_q = grad_q + jnp.einsum(
            "hqk,khd->qhd", dscores, near_k, preferred_element_type=jnp.float32
        )
        grad_k = jnp.einsum("hqk,qhd->khd", dscores, own_q, preferred_element_type=jnp.float32)
        grad_v = jnp.einsum(
            "hqk,qhd->khd", probs.astype(jnp.bfloat16), own_do, preferred_element_type=jnp.float32
        )
        stacked = jnp.concatenate(
            (grad_k.reshape(3, tile_rows, width), grad_v.reshape(3, tile_rows, width)), axis=1
        )
        return (grad_q, stacked)

    zeros = jnp.zeros((tile_rows, head_count, head_width), jnp.float32)
    grad_q, partial_sums = lax.scan(slab_step, zeros, (nearby, valid))
    folded = fold_back(partial_sums.reshape(3, 3, 3, 2 * tile_rows, width))
    grad_queries = grad_q.reshape(tile_rows, width) * score_scale
    grad_keys = folded[:tile_rows] * score_scale
    grad_values = folded[tile_rows:]
    return (
        grad_queries.astype(jnp.bfloat16).reshape(out_shape),
        grad_keys.astype(jnp.bfloat16).reshape(out_shape),
        grad_values.astype(jnp.bfloat16).reshape(out_shape),
    )


def arrived(ref, sem):
    pltpu.make_async_copy(ref, ref, sem).wait()


def window_kernel(
    rows,
    q_ref, k_ref, v_ref, o_ref, do_ref, log_ref,
    dq_ref, dk_ref, dv_ref,
    kv, qd, stat, stat_own, o_in, do_in, log_in, grads_out, grads_in, sums, dq_sum, dq_out, dq_in,
    final_kv, final_q,
    load_sem, kv_send, kv_recv, q_send, q_recv, halo_send, halo_recv,
    ret_send, ret_recv, dq_send, dq_recv, out_send, out_recv,
):
    f, r, b = lax.axis_index("frame"), lax.axis_index("row"), lax.axis_index("col")
    y, a = f // 2, f % 2
    tokens, width = q_ref.shape
    feats = width // 2
    scale = feats ** (-0.5)
    other_f = 2 * y + 1 - a
    across_f = f + 2 - 4 * y
    near = 1 - y
    has_row = {-1: r > 0, 1: r < rows - 1}

    barrier = pltpu.get_barrier_semaphore()

    def greet(where):
        pl.semaphore_signal(barrier, inc=1, device_id=where, device_id_type=MESH)

    for where in ((other_f, r, b), (f, r, 1 - b), (other_f, r, 1 - b), (across_f, r, b)):
        greet(where)
    for step in (-1, 1):
        @pl.when(has_row[step])
        def _():
            greet((f, r + step, b))
            greet((across_f, r + step, b))

    def cols(head):
        return pl.ds(pl.multiple_of(head * feats, feats), feats)

    def toks(frame):
        return pl.ds(pl.multiple_of(frame * tokens, 128), tokens)

    def remote(src, dst, send, recv, where):
        return pltpu.make_async_remote_copy(
            src_ref=src, dst_ref=dst, send_sem=send, recv_sem=recv, device_id=where, device_id_type=MESH
        )

    def q_slot(kind, frame, col):
        if kind == 2:
            return stat.at[col, :, toks(frame)]
        return qd.at[col, kind, toks(frame)]

    def q_source(kind, head):
        if kind == 2:
            return stat_own.at[head]
        return (q_ref, do_ref)[kind].at[:, cols(head)]

    def q_local(kind):
        pltpu.make_async_copy(q_source(kind, a), q_slot(kind, a, b), q_recv.at[b, a, kind]).start()

    def q_remote(kind, which):
        head, col = ((1 - a, b), (a, 1 - b), (1 - a, 1 - b))[which]
        remote(
            q_source(kind, head), q_slot(kind, a, b), q_send.at[which, kind], q_recv.at[b, a, kind],
            (2 * y + head, r, col),
        ).start()

    loads = [
        pltpu.make_async_copy(src, dst, load_sem.at[at])
        for at, (src, dst) in enumerate(((do_ref, do_in), (o_ref, o_in), (log_ref, log_in)))
    ]
    for kind, ref in enumerate((k_ref, v_ref)):
        pltpu.make_async_copy(ref.at[:, cols(a)], kv.at[1, a, kind], kv_recv.at[a, kind]).start()
    for load in loads:
        load.start()
    for kind in range(2):
        q_local(kind)

    for load in loads:
        load.wait()
    ones = jnp.ones((8, feats), jnp.bfloat16)
    along = (((1,), (1,)), ((), ()))
    for head in range(2):
        part = slice(head * feats, (head + 1) * feats)
        product = do_in[:, part].astype(jnp.float32) * o_in[:, part].astype(jnp.float32)
        high = product.astype(jnp.bfloat16)
        low = (product - high.astype(jnp.float32)).astype(jnp.bfloat16)
        delta = lax.dot_general(ones, high, along, preferred_element_type=jnp.float32)
        delta += lax.dot_general(ones, low, along, preferred_element_type=jnp.float32)
        stat_own[head] = delta
        stat_own[head, 0:1, :] = log_in[head : head + 1, :] * LOG2E
    q_local(2)

    pl.semaphore_wait(
        barrier, 4 + 2 * (has_row[-1].astype(jnp.int32) + has_row[1].astype(jnp.int32))
    )

    for kind, ref in enumerate((k_ref, v_ref)):
        remote(
            ref.at[:, cols(1 - a)], kv.at[1, a, kind], kv_send.at[kind], kv_recv.at[a, kind], (other_f, r, b)
        ).start()
    for which in range(3):
        for kind in (2, 0, 1):
            q_remote(kind, which)

    for frame in (a, 1 - a):
        for kind in range(2):
            arrived(kv.at[1, frame, kind], kv_recv.at[frame, kind])
        for step in (-1, 1):
            @pl.when(has_row[step])
            def _():
                remote(
                    kv.at[1, frame], kv.at[1 - step, frame], halo_send.at[1 - step, frame],
                    halo_recv.at[1 - step, frame], (f, r + step, b),
                ).start()

        @pl.when(near == frame)
        def _():
            remote(
                kv.at[1, frame], kv.at[1, 2], halo_send.at[1, 2], halo_recv.at[1, 2], (across_f, r, b)
            ).start()
            for step in (-1, 1):
                @pl.when(has_row[step])
                def _():
                    remote(
                        kv.at[1, frame], kv.at[1 - step, 2], halo_send.at[1 - step, 2],
                        halo_recv.at[1 - step, 2], (across_f, r + step, b),
                    ).start()

    dq_sum[...] = jnp.zeros_like(dq_sum)

    def is_outer(frame):
        return isinstance(frame, int) and frame == 2

    def one_block(at_row, at_frame, col, first):
        keys = kv[at_row, at_frame, 0]
        values = kv[at_row, at_frame, 1]
        keys_t = keys.T
        if is_outer(at_frame):
            chunks = [toks(near)]
        else:
            chunks = [pl.ds(at, 256) for at in range(0, 2 * tokens, 256)]

        def products(some):
            q_part = qd[col, 0, some, :]
            do_part = qd[col, 1, some, :]
            scores = lax.dot_general(keys, q_part, along, preferred_element_type=jnp.float32)
            dprobs = lax.dot_general(values, do_part, along, preferred_element_type=jnp.float32)
            return q_part, do_part, scores, dprobs

        dk = dv = None
        upcoming = products(chunks[0])
        for at, some in enumerate(chunks):
            q_part, do_part, scores, dprobs = upcoming
            if at + 1 < len(chunks):
                upcoming = products(chunks[at + 1])
            probs = jnp.exp2(scores * (scale * LOG2E) - stat[col, 0:1, some])
            dscores = probs * (dprobs - stat[col, 1:2, some])
            probs = probs.astype(jnp.bfloat16)
            dscores = dscores.astype(jnp.bfloat16)
            dv_part = jnp.dot(probs, do_part, preferred_element_type=jnp.float32)
            dk_part = jnp.dot(dscores, q_part, preferred_element_type=jnp.float32)
            dv = dv_part if dv is None else dv + dv_part
            dk = dk_part if dk is None else dk + dk_part
            dq_sum[col, :, some] += jnp.dot(keys_t, dscores, preferred_element_type=jnp.float32)
        if first:
            sums[at_row, at_frame, 0] = dk
            sums[at_row, at_frame, 1] = dv
        else:
            sums[at_row, at_frame, 0] += dk
            sums[at_row, at_frame, 1] += dv

    def give_back(at_row, at_frame):
        grads_out[at_row, at_frame] = sums[at_row, at_frame].astype(jnp.bfloat16)
        remote(
            grads_out.at[at_row, at_frame], grads_in.at[2 - at_row, at_frame],
            ret_send.at[at_row, at_frame], ret_recv.at[2 - at_row, at_frame],
            (across_f if is_outer(at_frame) else f, r + at_row - 1, b),
        ).start()

    def q_arrived(col):
        for frame in range(2):
            for kind in range(3):
                arrived(q_slot(kind, frame, col), q_recv.at[col, frame, kind])

    def own_row(col, first):
        def body(frame, carry):
            one_block(1, frame, col, first)
            return carry

        lax.fori_loop(0, 2, body, 0)

    def both_sides(frame, wait, blocks, back):
        def body(side, carry):
            at_row = 2 * side
            to_row = r + at_row - 1

            @pl.when((to_row >= 0) & (to_row < rows))
            def _():
                if wait:
                    arrived(kv.at[at_row, frame], halo_recv.at[at_row, frame])
                for col, first in blocks:
                    one_block(at_row, frame, col, first)
                if back:
                    give_back(at_row, frame)

            return carry

        lax.fori_loop(0, 2, body, 0)

    def send_dq(frame, which):
        dq_out[:, toks(frame)] = dq_sum[1 - b, :, toks(frame)].astype(jnp.bfloat16)
        remote(
            dq_out.at[:, toks(frame)], dq_in.at[:, toks(frame)], dq_send.at[which], dq_recv.at[which],
            (f, r, 1 - b),
        ).start()

    q_arrived(b)
    own_row(b, True)
    arrived(kv.at[1, 2], halo_recv.at[1, 2])
    one_block(1, 2, b, True)
    both_sides(a, True, ((b, True),), False)
    q_arrived(1 - b)
    both_sides(a, False, ((1 - b, False),), True)
    one_block(1, 2, 1 - b, False)
    give_back(1, 2)
    both_sides(1 - a, True, ((b, True), (1 - b, False)), True)
    both_sides(2, True, ((1 - b, True), (b, False)), True)
    own_row(1 - b, False)
    send_dq(1 - near, 0)
    send_dq(near, 1)

    def add_back(frame, at_row, at_frame):
        arrived(grads_in.at[at_row, at_frame], ret_recv.at[at_row, at_frame])
        sums[1, frame] += grads_in[at_row, at_frame].astype(jnp.float32)

    def finish_keys(frame):
        for step in (-1, 1):
            @pl.when(has_row[step])
            def _():
                add_back(frame, 1 + step, frame)

    def hand_out(kind, frame, src, ref):
        dst = ref.at[:, cols(a)]

        @pl.when(frame == a)
        def _():
            pltpu.make_async_copy(src, dst, out_recv.at[kind, a]).start()

        @pl.when(frame != a)
        def _():
            remote(src, dst, out_send.at[kind], out_recv.at[kind, a], (other_f, r, b)).start()

    def hand_out_keys(frame):
        final_kv[frame, 0] = (sums[1, frame, 0] * scale).astype(jnp.bfloat16)
        final_kv[frame, 1] = sums[1, frame, 1].astype(jnp.bfloat16)
        for kind, ref in ((1, dk_ref), (2, dv_ref)):
            hand_out(kind, frame, final_kv.at[frame, kind - 1], ref)

    def hand_out_queries(frame, which):
        arrived(dq_in.at[:, toks(frame)], dq_recv.at[which])
        total = dq_sum[b, :, toks(frame)] + dq_in[:, toks(frame)].astype(jnp.float32)
        final_q[toks(frame), :] = (total * scale).T.astype(jnp.bfloat16)
        hand_out(0, frame, final_q.at[toks(frame)], dq_ref)

    finish_keys(1 - near)
    hand_out_keys(1 - near)
    finish_keys(near)
    add_back(near, 1, 2)
    for step in (-1, 1):
        @pl.when(has_row[step])
        def _():
            add_back(near, 1 + step, 2)
    hand_out_keys(near)
    hand_out_queries(1 - near, 0)
    hand_out_queries(near, 1)

    for kind in range(3):
        out = (dq_ref, dk_ref, dv_ref)[kind]
        for head in range(2):
            arrived(out.at[:, head * feats : (head + 1) * feats], out_recv.at[kind, head])
        arrived(final_kv.at[0, 0], out_send.at[kind])
        for which in range(3):
            arrived(q_source(kind, 0), q_send.at[which, kind])
    for which in range(2):
        arrived(kv.at[1, 0, which], kv_send.at[which])
        arrived(dq_out.at[:, toks(0)], dq_send.at[which])
    arrived(kv.at[1, 2], halo_send.at[1, 2])
    arrived(grads_out.at[1, 2], ret_send.at[1, 2])
    for step in (-1, 1):
        @pl.when(has_row[step])
        def _():
            for frame in range(3):
                arrived(kv.at[1 - step, frame], halo_send.at[1 - step, frame])
                arrived(grads_out.at[1 + step, frame], ret_send.at[1 + step, frame])


def copy_kernel(*refs):
    sems = refs[6]
    copies = [pltpu.make_async_copy(refs[at], refs[3 + at], sems.at[at]) for at in range(3)]
    for copy in copies:
        copy.start()
    for copy in copies:
        copy.wait()


def local_window(rows, queries, key_vectors, value_vectors, forward_out, cotangent, log_norm):
    shape = queries.shape
    tokens, width = shape[3:]
    feats = width // 2
    flat = [x.reshape(tokens, width) for x in (queries, key_vectors, value_vectors, forward_out, cotangent)]
    half = (tokens, feats)
    low, full = jnp.bfloat16, jnp.float32
    dma = pltpu.SemaphoreType.DMA
    any_space = pl.BlockSpec(memory_space=pl.ANY)
    outs = pl.pallas_call(
        functools.partial(window_kernel, rows),
        out_shape=[jax.ShapeDtypeStruct((tokens, width), low)] * 3,
        in_specs=[any_space] * 6,
        out_specs=[any_space] * 3,
        scratch_shapes=[
            pltpu.VMEM((3, 3, 2) + half, low),
            pltpu.VMEM((2, 2, 2 * tokens, feats), low),
            pltpu.VMEM((2, 8, 2 * tokens), full),
            pltpu.VMEM((2, 8, tokens), full),
            pltpu.VMEM((tokens, width), low),
            pltpu.VMEM((tokens, width), low),
            pltpu.VMEM((2, tokens), full),
            pltpu.VMEM((3, 3, 2) + half, low),
            pltpu.VMEM((3, 3, 2) + half, low),
            pltpu.VMEM((3, 3, 2) + half, full),
            pltpu.VMEM((2, feats, 2 * tokens), full),
            pltpu.VMEM((feats, 2 * tokens), low),
            pltpu.VMEM((feats, 2 * tokens), low),
            pltpu.VMEM((2, 2) + half, low),
            pltpu.VMEM((2 * tokens, feats), low),
            dma((3,)), dma((2,)), dma((2, 2)), dma((3, 3)), dma((2, 2, 3)), dma((3, 3)), dma((3, 3)),
            dma((3, 3)), dma((3, 3)), dma((2,)), dma((2,)), dma((3,)), dma((3, 2)),
        ],
        compiler_params=pltpu.CompilerParams(
            collective_id=0, has_side_effects=True, vmem_limit_bytes=60 * 2**20
        ),
    )(*flat, log_norm.reshape(2, tokens))
    outs = pl.pallas_call(
        copy_kernel,
        out_shape=[jax.ShapeDtypeStruct((tokens, width), low)] * 3,
        in_specs=[any_space] * 3,
        out_specs=[any_space] * 3,
        scratch_shapes=[dma((3,))],
    )(*outs)
    return tuple(x.reshape(shape) for x in outs)


def solution(mesh):
    placed = (P("frame", "row", "col", None, None),) * 6
    sizes = dict(mesh.shape)
    body = local
    if sizes["frame"] == 4 and sizes["col"] == 2:
        body = functools.partial(local_window, sizes["row"])
    return jax.shard_map(
        body,
        mesh=mesh,
        in_specs=placed,
        out_specs=placed[:3],
        check_vma=False,
    )
```

```python
import functools

import jax
import jax.numpy as jnp
from jax import lax
from jax.experimental import pallas as pl
from jax.experimental.pallas import tpu as pltpu
from jax.sharding import PartitionSpec as P

MESH = pl.DeviceIdType.MESH
LOG2E = 1.4426950408889634


def passed_along(x, axis, by):
    peers = lax.axis_size(axis)
    pairs = [(i, i + by) for i in range(peers) if 0 <= i + by < peers]
    return lax.ppermute(x, axis, pairs)


def with_halo(x, sides, width):
    for axis, dim in sides:
        peers, length = (lax.axis_size(axis), x.shape[dim])
        up = [(i, (i + 1) % peers) for i in range(peers - 1)]
        down = [(j, i) for i, j in up]
        last = lax.slice_in_dim(x, length - width, length, axis=dim)
        leading = lax.slice_in_dim(x, 0, width, axis=dim)
        before = lax.ppermute(last, axis, up)
        after = lax.ppermute(leading, axis, down)
        x = jnp.concatenate([before, x, after], axis=dim)
    return x


def window_valid():
    offsets = jnp.arange(3, dtype=jnp.int32) - 1
    frame_pos = lax.axis_index("frame") + offsets
    row_pos = lax.axis_index("row") + offsets
    col_pos = lax.axis_index("col") + offsets
    along_f = (frame_pos >= 0) & (frame_pos < lax.axis_size("frame"))
    along_r = (row_pos >= 0) & (row_pos < lax.axis_size("row"))
    along_c = (col_pos >= 0) & (col_pos < lax.axis_size("col"))
    return along_f[:, None, None] & along_r[None, :, None] & along_c[None, None, :]


def reduce_frame(partial_sums, dim):
    from_next = passed_along(lax.index_in_dim(partial_sums, 0, dim, keepdims=False), "frame", -1)
    from_prev = passed_along(lax.index_in_dim(partial_sums, 2, dim, keepdims=False), "frame", 1)
    return lax.index_in_dim(partial_sums, 1, dim, keepdims=False) + from_next + from_prev


def reduce_row(partial_sums, dim):
    from_next = passed_along(lax.index_in_dim(partial_sums, 0, dim, keepdims=False), "row", -1)
    from_prev = passed_along(lax.index_in_dim(partial_sums, 2, dim, keepdims=False), "row", 1)
    return lax.index_in_dim(partial_sums, 1, dim, keepdims=False) + from_next + from_prev


def reduce_col(partial_sums, dim):
    from_next = passed_along(lax.index_in_dim(partial_sums, 0, dim, keepdims=False), "col", -1)
    from_prev = passed_along(lax.index_in_dim(partial_sums, 2, dim, keepdims=False), "col", 1)
    return lax.index_in_dim(partial_sums, 1, dim, keepdims=False) + from_next + from_prev


def fold_back(partial_sums):
    partial_sums = reduce_frame(partial_sums, 0)
    partial_sums = reduce_row(partial_sums, 0)
    return reduce_col(partial_sums, 0)


def local(queries, key_vectors, value_vectors, forward_out, cotangent, log_norm):
    tile_rows = queries.shape[3]
    width = queries.shape[4]
    head_count = log_norm.shape[3]
    head_width = width // head_count
    score_scale = head_width ** (-0.5)
    valid = window_valid().reshape(9, 3)
    own_q = queries.reshape(tile_rows, head_count, head_width)
    own_do = cotangent.reshape(tile_rows, head_count, head_width)
    products = cotangent.astype(jnp.float32) * forward_out.astype(jnp.float32)
    row_delta = jnp.sum(products.reshape(tile_rows, head_count, head_width), axis=-1).T
    own_log = log_norm.reshape(head_count, tile_rows)
    out_shape = (1, 1, 1, tile_rows, width)
    joined = jnp.concatenate((key_vectors, value_vectors), axis=3)
    nearby = with_halo(joined, (("frame", 0), ("row", 1), ("col", 2)), 1)
    nearby = nearby.reshape(9, 3, 2 * tile_rows, width)

    def slab_step(grad_q, inputs):
        slab, valid_slab = inputs
        near_k = slab[:, :tile_rows].reshape(3 * tile_rows, head_count, head_width)
        near_v = slab[:, tile_rows:].reshape(3 * tile_rows, head_count, head_width)
        keep = jnp.repeat(valid_slab, tile_rows)
        scores = (
            jnp.einsum("qhd,khd->hqk", own_q, near_k, preferred_element_type=jnp.float32)
            * score_scale
        )
        probs = jnp.where(keep[None, None, :], jnp.exp(scores - own_log[:, :, None]), 0.0)
        dprobs = jnp.einsum("qhd,khd->hqk", own_do, near_v, preferred_element_type=jnp.float32)
        dscores = (probs * (dprobs - row_delta[:, :, None])).astype(jnp.bfloat16)
        grad_q = grad_q + jnp.einsum(
            "hqk,khd->qhd", dscores, near_k, preferred_element_type=jnp.float32
        )
        grad_k = jnp.einsum("hqk,qhd->khd", dscores, own_q, preferred_element_type=jnp.float32)
        grad_v = jnp.einsum(
            "hqk,qhd->khd", probs.astype(jnp.bfloat16), own_do, preferred_element_type=jnp.float32
        )
        stacked = jnp.concatenate(
            (grad_k.reshape(3, tile_rows, width), grad_v.reshape(3, tile_rows, width)), axis=1
        )
        return (grad_q, stacked)

    zeros = jnp.zeros((tile_rows, head_count, head_width), jnp.float32)
    grad_q, partial_sums = lax.scan(slab_step, zeros, (nearby, valid))
    folded = fold_back(partial_sums.reshape(3, 3, 3, 2 * tile_rows, width))
    grad_queries = grad_q.reshape(tile_rows, width) * score_scale
    grad_keys = folded[:tile_rows] * score_scale
    grad_values = folded[tile_rows:]
    return (
        grad_queries.astype(jnp.bfloat16).reshape(out_shape),
        grad_keys.astype(jnp.bfloat16).reshape(out_shape),
        grad_values.astype(jnp.bfloat16).reshape(out_shape),
    )


def arrived(ref, sem):
    pltpu.make_async_copy(ref, ref, sem).wait()


def window_kernel(
    rows,
    q_ref, k_ref, v_ref, o_ref, do_ref, log_ref,
    dq_ref, dk_ref, dv_ref,
    kv, qd, stat, stat_own, o_in, do_in, log_in, grads_out, grads_in, sums, dq_sum, dq_out, dq_in,
    final_kv, final_q,
    load_sem, kv_send, kv_recv, q_send, q_recv, halo_send, halo_recv,
    ret_send, ret_recv, dq_send, dq_recv, out_send, out_recv,
):
    f, r, b = lax.axis_index("frame"), lax.axis_index("row"), lax.axis_index("col")
    y, a = f // 2, f % 2
    tokens, width = q_ref.shape
    feats = width // 2
    scale = feats ** (-0.5)
    other_f = 2 * y + 1 - a
    across_f = f + 2 - 4 * y
    near = 1 - y
    has_row = {-1: r > 0, 1: r < rows - 1}

    barrier = pltpu.get_barrier_semaphore()

    def greet(where):
        pl.semaphore_signal(barrier, inc=1, device_id=where, device_id_type=MESH)

    for where in ((other_f, r, b), (f, r, 1 - b), (other_f, r, 1 - b), (across_f, r, b)):
        greet(where)
    for step in (-1, 1):
        @pl.when(has_row[step])
        def _():
            greet((f, r + step, b))
            greet((across_f, r + step, b))

    def cols(head):
        return pl.ds(pl.multiple_of(head * feats, feats), feats)

    def toks(frame):
        return pl.ds(pl.multiple_of(frame * tokens, 128), tokens)

    def remote(src, dst, send, recv, where):
        return pltpu.make_async_remote_copy(
            src_ref=src, dst_ref=dst, send_sem=send, recv_sem=recv, device_id=where, device_id_type=MESH
        )

    def q_slot(kind, frame, col):
        if kind == 2:
            return stat.at[col, :, toks(frame)]
        return qd.at[col, kind, toks(frame)]

    def q_source(kind, head):
        if kind == 2:
            return stat_own.at[head]
        return (q_ref, do_ref)[kind].at[:, cols(head)]

    def q_local(kind):
        pltpu.make_async_copy(q_source(kind, a), q_slot(kind, a, b), q_recv.at[b, a, kind]).start()

    def q_remote(kind, which):
        head, col = ((1 - a, b), (a, 1 - b), (1 - a, 1 - b))[which]
        remote(
            q_source(kind, head), q_slot(kind, a, b), q_send.at[which, kind], q_recv.at[b, a, kind],
            (2 * y + head, r, col),
        ).start()

    loads = [
        pltpu.make_async_copy(src, dst, load_sem.at[at])
        for at, (src, dst) in enumerate(((do_ref, do_in), (o_ref, o_in), (log_ref, log_in)))
    ]
    for kind, ref in enumerate((k_ref, v_ref)):
        pltpu.make_async_copy(ref.at[:, cols(a)], kv.at[1, a, kind], kv_recv.at[a, kind]).start()
    for load in loads:
        load.start()
    for kind in range(2):
        q_local(kind)

    for load in loads:
        load.wait()
    ones = jnp.ones((8, feats), jnp.bfloat16)
    along = (((1,), (1,)), ((), ()))
    for head in range(2):
        part = slice(head * feats, (head + 1) * feats)
        product = do_in[:, part].astype(jnp.float32) * o_in[:, part].astype(jnp.float32)
        high = product.astype(jnp.bfloat16)
        low = (product - high.astype(jnp.float32)).astype(jnp.bfloat16)
        delta = lax.dot_general(ones, high, along, preferred_element_type=jnp.float32)
        delta += lax.dot_general(ones, low, along, preferred_element_type=jnp.float32)
        stat_own[head] = delta
        stat_own[head, 0:1, :] = log_in[head : head + 1, :] * LOG2E
    q_local(2)

    pl.semaphore_wait(
        barrier, 4 + 2 * (has_row[-1].astype(jnp.int32) + has_row[1].astype(jnp.int32))
    )

    for kind, ref in enumerate((k_ref, v_ref)):
        remote(
            ref.at[:, cols(1 - a)], kv.at[1, a, kind], kv_send.at[kind], kv_recv.at[a, kind], (other_f, r, b)
        ).start()
    for which in range(3):
        for kind in (2, 0, 1):
            q_remote(kind, which)

    for frame in (a, 1 - a):
        for kind in range(2):
            arrived(kv.at[1, frame, kind], kv_recv.at[frame, kind])
        for step in (-1, 1):
            @pl.when(has_row[step])
            def _():
                remote(
                    kv.at[1, frame], kv.at[1 - step, frame], halo_send.at[1 - step, frame],
                    halo_recv.at[1 - step, frame], (f, r + step, b),
                ).start()

        @pl.when(near == frame)
        def _():
            remote(
                kv.at[1, frame], kv.at[1, 2], halo_send.at[1, 2], halo_recv.at[1, 2], (across_f, r, b)
            ).start()
            for step in (-1, 1):
                @pl.when(has_row[step])
                def _():
                    remote(
                        kv.at[1, frame], kv.at[1 - step, 2], halo_send.at[1 - step, 2],
                        halo_recv.at[1 - step, 2], (across_f, r + step, b),
                    ).start()

    dq_sum[...] = jnp.zeros_like(dq_sum)

    def is_outer(frame):
        return isinstance(frame, int) and frame == 2

    def one_block(at_row, at_frame, col, first):
        keys = kv[at_row, at_frame, 0]
        values = kv[at_row, at_frame, 1]
        keys_t = keys.T
        if is_outer(at_frame):
            chunks = [toks(near)]
        else:
            chunks = [pl.ds(at, 256) for at in range(0, 2 * tokens, 256)]

        all_probs, all_dscores = [], []
        for some in chunks:
            scores = lax.dot_general(keys, qd[col, 0, some, :], along, preferred_element_type=jnp.float32)
            dprobs = lax.dot_general(values, qd[col, 1, some, :], along, preferred_element_type=jnp.float32)
            probs = jnp.exp2(scores * (scale * LOG2E) - stat[col, 0:1, some])
            dscores = (probs * (dprobs - stat[col, 1:2, some])).astype(jnp.bfloat16)
            dq_sum[col, :, some] += jnp.dot(keys_t, dscores, preferred_element_type=jnp.float32)
            all_probs.append(probs.astype(jnp.bfloat16))
            all_dscores.append(dscores)
        together = chunks[0] if len(chunks) == 1 else pl.ds(0, 2 * tokens)
        dv = jnp.dot(
            jnp.concatenate(all_probs, axis=1), qd[col, 1, together, :], preferred_element_type=jnp.float32
        )
        dk = jnp.dot(
            jnp.concatenate(all_dscores, axis=1), qd[col, 0, together, :], preferred_element_type=jnp.float32
        )
        if first:
            sums[at_row, at_frame, 0] = dk
            sums[at_row, at_frame, 1] = dv
        else:
            sums[at_row, at_frame, 0] += dk
            sums[at_row, at_frame, 1] += dv

    def give_back(at_row, at_frame):
        grads_out[at_row, at_frame] = sums[at_row, at_frame].astype(jnp.bfloat16)
        remote(
            grads_out.at[at_row, at_frame], grads_in.at[2 - at_row, at_frame],
            ret_send.at[at_row, at_frame], ret_recv.at[2 - at_row, at_frame],
            (across_f if is_outer(at_frame) else f, r + at_row - 1, b),
        ).start()

    def q_arrived(col):
        for frame in range(2):
            for kind in range(3):
                arrived(q_slot(kind, frame, col), q_recv.at[col, frame, kind])

    def own_row(col, first):
        def body(frame, carry):
            one_block(1, frame, col, first)
            return carry

        lax.fori_loop(0, 2, body, 0)

    def both_sides(frame, wait, blocks, back):
        def body(side, carry):
            at_row = 2 * side
            to_row = r + at_row - 1

            @pl.when((to_row >= 0) & (to_row < rows))
            def _():
                if wait:
                    arrived(kv.at[at_row, frame], halo_recv.at[at_row, frame])
                for col, first in blocks:
                    one_block(at_row, frame, col, first)
                if back:
                    give_back(at_row, frame)

            return carry

        lax.fori_loop(0, 2, body, 0)

    def send_dq(frame, which):
        dq_out[:, toks(frame)] = dq_sum[1 - b, :, toks(frame)].astype(jnp.bfloat16)
        remote(
            dq_out.at[:, toks(frame)], dq_in.at[:, toks(frame)], dq_send.at[which], dq_recv.at[which],
            (f, r, 1 - b),
        ).start()

    q_arrived(b)
    own_row(b, True)
    arrived(kv.at[1, 2], halo_recv.at[1, 2])
    one_block(1, 2, b, True)
    both_sides(a, True, ((b, True),), False)
    q_arrived(1 - b)
    both_sides(a, False, ((1 - b, False),), True)
    one_block(1, 2, 1 - b, False)
    give_back(1, 2)
    both_sides(1 - a, True, ((b, True), (1 - b, False)), True)
    both_sides(2, True, ((1 - b, True), (b, False)), True)
    own_row(1 - b, False)
    send_dq(1 - near, 0)
    send_dq(near, 1)

    def add_back(frame, at_row, at_frame):
        arrived(grads_in.at[at_row, at_frame], ret_recv.at[at_row, at_frame])
        sums[1, frame] += grads_in[at_row, at_frame].astype(jnp.float32)

    def finish_keys(frame):
        for step in (-1, 1):
            @pl.when(has_row[step])
            def _():
                add_back(frame, 1 + step, frame)

    def hand_out(kind, frame, src, ref):
        dst = ref.at[:, cols(a)]

        @pl.when(frame == a)
        def _():
            pltpu.make_async_copy(src, dst, out_recv.at[kind, a]).start()

        @pl.when(frame != a)
        def _():
            remote(src, dst, out_send.at[kind], out_recv.at[kind, a], (other_f, r, b)).start()

    def hand_out_keys(frame):
        final_kv[frame, 0] = (sums[1, frame, 0] * scale).astype(jnp.bfloat16)
        final_kv[frame, 1] = sums[1, frame, 1].astype(jnp.bfloat16)
        for kind, ref in ((1, dk_ref), (2, dv_ref)):
            hand_out(kind, frame, final_kv.at[frame, kind - 1], ref)

    def hand_out_queries(frame, which):
        arrived(dq_in.at[:, toks(frame)], dq_recv.at[which])
        total = dq_sum[b, :, toks(frame)] + dq_in[:, toks(frame)].astype(jnp.float32)
        final_q[toks(frame), :] = (total * scale).T.astype(jnp.bfloat16)
        hand_out(0, frame, final_q.at[toks(frame)], dq_ref)

    finish_keys(1 - near)
    hand_out_keys(1 - near)
    finish_keys(near)
    add_back(near, 1, 2)
    for step in (-1, 1):
        @pl.when(has_row[step])
        def _():
            add_back(near, 1 + step, 2)
    hand_out_keys(near)
    hand_out_queries(1 - near, 0)
    hand_out_queries(near, 1)

    for kind in range(3):
        out = (dq_ref, dk_ref, dv_ref)[kind]
        for head in range(2):
            arrived(out.at[:, head * feats : (head + 1) * feats], out_recv.at[kind, head])
        arrived(final_kv.at[0, 0], out_send.at[kind])
        for which in range(3):
            arrived(q_source(kind, 0), q_send.at[which, kind])
    for which in range(2):
        arrived(kv.at[1, 0, which], kv_send.at[which])
        arrived(dq_out.at[:, toks(0)], dq_send.at[which])
    arrived(kv.at[1, 2], halo_send.at[1, 2])
    arrived(grads_out.at[1, 2], ret_send.at[1, 2])
    for step in (-1, 1):
        @pl.when(has_row[step])
        def _():
            for frame in range(3):
                arrived(kv.at[1 - step, frame], halo_send.at[1 - step, frame])
                arrived(grads_out.at[1 + step, frame], ret_send.at[1 + step, frame])


def copy_kernel(*refs):
    sems = refs[6]
    copies = [pltpu.make_async_copy(refs[at], refs[3 + at], sems.at[at]) for at in range(3)]
    for copy in copies:
        copy.start()
    for copy in copies:
        copy.wait()


def local_window(rows, queries, key_vectors, value_vectors, forward_out, cotangent, log_norm):
    shape = queries.shape
    tokens, width = shape[3:]
    feats = width // 2
    flat = [x.reshape(tokens, width) for x in (queries, key_vectors, value_vectors, forward_out, cotangent)]
    half = (tokens, feats)
    low, full = jnp.bfloat16, jnp.float32
    dma = pltpu.SemaphoreType.DMA
    any_space = pl.BlockSpec(memory_space=pl.ANY)
    vmem = pl.BlockSpec(memory_space=pltpu.VMEM)
    outs = pl.pallas_call(
        functools.partial(window_kernel, rows),
        out_shape=[jax.ShapeDtypeStruct((tokens, width), low)] * 3,
        in_specs=[any_space] * 6,
        out_specs=[any_space] * 3,
        scratch_shapes=[
            pltpu.VMEM((3, 3, 2) + half, low),
            pltpu.VMEM((2, 2, 2 * tokens, feats), low),
            pltpu.VMEM((2, 8, 2 * tokens), full),
            pltpu.VMEM((2, 8, tokens), full),
            pltpu.VMEM((tokens, width), low),
            pltpu.VMEM((tokens, width), low),
            pltpu.VMEM((2, tokens), full),
            pltpu.VMEM((3, 3, 2) + half, low),
            pltpu.VMEM((3, 3, 2) + half, low),
            pltpu.VMEM((3, 3, 2) + half, full),
            pltpu.VMEM((2, feats, 2 * tokens), full),
            pltpu.VMEM((feats, 2 * tokens), low),
            pltpu.VMEM((feats, 2 * tokens), low),
            pltpu.VMEM((2, 2) + half, low),
            pltpu.VMEM((2 * tokens, feats), low),
            dma((3,)), dma((2,)), dma((2, 2)), dma((3, 3)), dma((2, 2, 3)), dma((3, 3)), dma((3, 3)),
            dma((3, 3)), dma((3, 3)), dma((2,)), dma((2,)), dma((3,)), dma((3, 2)),
        ],
        compiler_params=pltpu.CompilerParams(
            collective_id=0, has_side_effects=True, vmem_limit_bytes=60 * 2**20
        ),
    )(*flat, log_norm.reshape(2, tokens))
    outs = pl.pallas_call(
        copy_kernel,
        out_shape=[jax.ShapeDtypeStruct((tokens, width), low)] * 3,
        in_specs=[vmem] * 3,
        out_specs=[any_space] * 3,
        scratch_shapes=[dma((3,))],
    )(*outs)
    return tuple(x.reshape(shape) for x in outs)


def solution(mesh):
    placed = (P("frame", "row", "col", None, None),) * 6
    sizes = dict(mesh.shape)
    body = local
    if sizes["frame"] == 4 and sizes["col"] == 2:
        body = functools.partial(local_window, sizes["row"])
    return jax.shard_map(
        body,
        mesh=mesh,
        in_specs=placed,
        out_specs=placed[:3],
        check_vma=False,
    )
```

```python
import functools

import jax
import jax.numpy as jnp
from jax import lax
from jax.experimental import pallas as pl
from jax.experimental.pallas import tpu as pltpu
from jax.sharding import PartitionSpec as P

MESH = pl.DeviceIdType.MESH
LOG2E = 1.4426950408889634


def passed_along(x, axis, by):
    peers = lax.axis_size(axis)
    pairs = [(i, i + by) for i in range(peers) if 0 <= i + by < peers]
    return lax.ppermute(x, axis, pairs)


def with_halo(x, sides, width):
    for axis, dim in sides:
        peers, length = (lax.axis_size(axis), x.shape[dim])
        up = [(i, (i + 1) % peers) for i in range(peers - 1)]
        down = [(j, i) for i, j in up]
        last = lax.slice_in_dim(x, length - width, length, axis=dim)
        leading = lax.slice_in_dim(x, 0, width, axis=dim)
        before = lax.ppermute(last, axis, up)
        after = lax.ppermute(leading, axis, down)
        x = jnp.concatenate([before, x, after], axis=dim)
    return x


def window_valid():
    offsets = jnp.arange(3, dtype=jnp.int32) - 1
    frame_pos = lax.axis_index("frame") + offsets
    row_pos = lax.axis_index("row") + offsets
    col_pos = lax.axis_index("col") + offsets
    along_f = (frame_pos >= 0) & (frame_pos < lax.axis_size("frame"))
    along_r = (row_pos >= 0) & (row_pos < lax.axis_size("row"))
    along_c = (col_pos >= 0) & (col_pos < lax.axis_size("col"))
    return along_f[:, None, None] & along_r[None, :, None] & along_c[None, None, :]


def reduce_frame(partial_sums, dim):
    from_next = passed_along(lax.index_in_dim(partial_sums, 0, dim, keepdims=False), "frame", -1)
    from_prev = passed_along(lax.index_in_dim(partial_sums, 2, dim, keepdims=False), "frame", 1)
    return lax.index_in_dim(partial_sums, 1, dim, keepdims=False) + from_next + from_prev


def reduce_row(partial_sums, dim):
    from_next = passed_along(lax.index_in_dim(partial_sums, 0, dim, keepdims=False), "row", -1)
    from_prev = passed_along(lax.index_in_dim(partial_sums, 2, dim, keepdims=False), "row", 1)
    return lax.index_in_dim(partial_sums, 1, dim, keepdims=False) + from_next + from_prev


def reduce_col(partial_sums, dim):
    from_next = passed_along(lax.index_in_dim(partial_sums, 0, dim, keepdims=False), "col", -1)
    from_prev = passed_along(lax.index_in_dim(partial_sums, 2, dim, keepdims=False), "col", 1)
    return lax.index_in_dim(partial_sums, 1, dim, keepdims=False) + from_next + from_prev


def fold_back(partial_sums):
    partial_sums = reduce_frame(partial_sums, 0)
    partial_sums = reduce_row(partial_sums, 0)
    return reduce_col(partial_sums, 0)


def local(queries, key_vectors, value_vectors, forward_out, cotangent, log_norm):
    tile_rows = queries.shape[3]
    width = queries.shape[4]
    head_count = log_norm.shape[3]
    head_width = width // head_count
    score_scale = head_width ** (-0.5)
    valid = window_valid().reshape(9, 3)
    own_q = queries.reshape(tile_rows, head_count, head_width)
    own_do = cotangent.reshape(tile_rows, head_count, head_width)
    products = cotangent.astype(jnp.float32) * forward_out.astype(jnp.float32)
    row_delta = jnp.sum(products.reshape(tile_rows, head_count, head_width), axis=-1).T
    own_log = log_norm.reshape(head_count, tile_rows)
    out_shape = (1, 1, 1, tile_rows, width)
    joined = jnp.concatenate((key_vectors, value_vectors), axis=3)
    nearby = with_halo(joined, (("frame", 0), ("row", 1), ("col", 2)), 1)
    nearby = nearby.reshape(9, 3, 2 * tile_rows, width)

    def slab_step(grad_q, inputs):
        slab, valid_slab = inputs
        near_k = slab[:, :tile_rows].reshape(3 * tile_rows, head_count, head_width)
        near_v = slab[:, tile_rows:].reshape(3 * tile_rows, head_count, head_width)
        keep = jnp.repeat(valid_slab, tile_rows)
        scores = (
            jnp.einsum("qhd,khd->hqk", own_q, near_k, preferred_element_type=jnp.float32)
            * score_scale
        )
        probs = jnp.where(keep[None, None, :], jnp.exp(scores - own_log[:, :, None]), 0.0)
        dprobs = jnp.einsum("qhd,khd->hqk", own_do, near_v, preferred_element_type=jnp.float32)
        dscores = (probs * (dprobs - row_delta[:, :, None])).astype(jnp.bfloat16)
        grad_q = grad_q + jnp.einsum(
            "hqk,khd->qhd", dscores, near_k, preferred_element_type=jnp.float32
        )
        grad_k = jnp.einsum("hqk,qhd->khd", dscores, own_q, preferred_element_type=jnp.float32)
        grad_v = jnp.einsum(
            "hqk,qhd->khd", probs.astype(jnp.bfloat16), own_do, preferred_element_type=jnp.float32
        )
        stacked = jnp.concatenate(
            (grad_k.reshape(3, tile_rows, width), grad_v.reshape(3, tile_rows, width)), axis=1
        )
        return (grad_q, stacked)

    zeros = jnp.zeros((tile_rows, head_count, head_width), jnp.float32)
    grad_q, partial_sums = lax.scan(slab_step, zeros, (nearby, valid))
    folded = fold_back(partial_sums.reshape(3, 3, 3, 2 * tile_rows, width))
    grad_queries = grad_q.reshape(tile_rows, width) * score_scale
    grad_keys = folded[:tile_rows] * score_scale
    grad_values = folded[tile_rows:]
    return (
        grad_queries.astype(jnp.bfloat16).reshape(out_shape),
        grad_keys.astype(jnp.bfloat16).reshape(out_shape),
        grad_values.astype(jnp.bfloat16).reshape(out_shape),
    )


def arrived(ref, sem):
    pltpu.make_async_copy(ref, ref, sem).wait()


def window_kernel(
    rows,
    q_ref, k_ref, v_ref, o_ref, do_ref, log_ref,
    dq_ref, dk_ref, dv_ref,
    kv, qd, turned, stat, stat_own, o_in, do_in, log_in, grads_out, grads_in, sums, dq_sum, dq_out, dq_in,
    final_kv, final_q,
    load_sem, kv_send, kv_recv, q_send, q_recv, halo_send, halo_recv, corner_send, corner_recv,
    ret_send, ret_recv, dq_send, dq_recv, out_send, out_recv,
):
    f, r, b = lax.axis_index("frame"), lax.axis_index("row"), lax.axis_index("col")
    y, a = f // 2, f % 2
    tokens, width = q_ref.shape
    feats = width // 2
    scale = feats ** (-0.5)
    other_f = 2 * y + 1 - a
    across_f = f + 2 - 4 * y
    near = 1 - y
    has_row = {-1: r > 0, 1: r < rows - 1}

    barrier = pltpu.get_barrier_semaphore()

    def greet(where):
        pl.semaphore_signal(barrier, inc=1, device_id=where, device_id_type=MESH)

    for where in ((other_f, r, b), (f, r, 1 - b), (other_f, r, 1 - b), (across_f, r, b)):
        greet(where)
    for step in (-1, 1):
        @pl.when(has_row[step])
        def _():
            greet((f, r + step, b))
            greet((across_f, r + step, b))

    def cols(head):
        return pl.ds(pl.multiple_of(head * feats, feats), feats)

    def toks(frame):
        return pl.ds(pl.multiple_of(frame * tokens, 128), tokens)

    def remote(src, dst, send, recv, where):
        return pltpu.make_async_remote_copy(
            src_ref=src, dst_ref=dst, send_sem=send, recv_sem=recv, device_id=where, device_id_type=MESH
        )

    def q_slot(kind, frame, col):
        if kind == 2:
            return stat.at[col, :, toks(frame)]
        return qd.at[col, kind, toks(frame)]

    def q_source(kind, head):
        if kind == 2:
            return stat_own.at[head]
        return (q_ref, do_ref)[kind].at[:, cols(head)]

    def q_local(kind):
        pltpu.make_async_copy(q_source(kind, a), q_slot(kind, a, b), q_recv.at[b, a, kind]).start()

    def q_remote(kind, which):
        head, col = ((1 - a, b), (a, 1 - b), (1 - a, 1 - b))[which]
        remote(
            q_source(kind, head), q_slot(kind, a, b), q_send.at[which, kind], q_recv.at[b, a, kind],
            (2 * y + head, r, col),
        ).start()

    loads = [
        pltpu.make_async_copy(src, dst, load_sem.at[at])
        for at, (src, dst) in enumerate(((do_ref, do_in), (o_ref, o_in), (log_ref, log_in)))
    ]
    for kind, ref in enumerate((k_ref, v_ref)):
        pltpu.make_async_copy(ref.at[:, cols(a)], kv.at[1, a, kind], kv_recv.at[a, kind]).start()
    for load in loads:
        load.start()
    for kind in range(2):
        q_local(kind)

    for load in loads:
        load.wait()
    ones = jnp.ones((8, feats), jnp.bfloat16)
    along = (((1,), (1,)), ((), ()))
    for head in range(2):
        part = slice(head * feats, (head + 1) * feats)
        product = do_in[:, part].astype(jnp.float32) * o_in[:, part].astype(jnp.float32)
        high = product.astype(jnp.bfloat16)
        low = (product - high.astype(jnp.float32)).astype(jnp.bfloat16)
        delta = lax.dot_general(ones, high, along, preferred_element_type=jnp.float32)
        delta += lax.dot_general(ones, low, along, preferred_element_type=jnp.float32)
        stat_own[head] = delta
        stat_own[head, 0:1, :] = log_in[head : head + 1, :] * LOG2E
    q_local(2)

    pl.semaphore_wait(
        barrier, 4 + 2 * (has_row[-1].astype(jnp.int32) + has_row[1].astype(jnp.int32))
    )

    for kind, ref in enumerate((k_ref, v_ref)):
        remote(
            ref.at[:, cols(1 - a)], kv.at[1, a, kind], kv_send.at[kind], kv_recv.at[a, kind], (other_f, r, b)
        ).start()
    for which in range(3):
        for kind in (2, 0, 1):
            q_remote(kind, which)

    for frame in (near, 1 - near):
        for kind in range(2):
            arrived(kv.at[1, frame, kind], kv_recv.at[frame, kind])
        if frame is near:
            remote(
                kv.at[1, frame], kv.at[1, 2], halo_send.at[1, 2], halo_recv.at[1, 2], (across_f, r, b)
            ).start()
        for step in (-1, 1):
            @pl.when(has_row[step])
            def _():
                remote(
                    kv.at[1, frame], kv.at[1 - step, frame], halo_send.at[1 - step, frame],
                    halo_recv.at[1 - step, frame], (f, r + step, b),
                ).start()

    dq_sum[...] = jnp.zeros_like(dq_sum)

    def is_outer(frame):
        return isinstance(frame, int) and frame == 2

    by_row, by_frame = pl.ds(0, tokens // 3), pl.ds(tokens // 3, tokens - tokens // 3)

    def pass_corners():
        arrived(kv.at[1, 2], halo_recv.at[1, 2])
        for step in (-1, 1):
            @pl.when(has_row[step])
            def _():
                remote(
                    kv.at[1, 2, :, by_row], kv.at[1 - step, 2, :, by_row], halo_send.at[1 - step, 2],
                    corner_recv.at[1 - step, 0], (f, r + step, b),
                ).start()
        for step in (-1, 1):
            @pl.when(has_row[step])
            def _():
                arrived(kv.at[1 + step, near], halo_recv.at[1 + step, near])
                remote(
                    kv.at[1 + step, near, :, by_frame], kv.at[1 + step, 2, :, by_frame],
                    corner_send.at[1 + step], corner_recv.at[1 + step, 1], (across_f, r, b),
                ).start()

    def one_block(at_row, at_frame, col, first):
        keys = kv[at_row, at_frame, 0]
        values = kv[at_row, at_frame, 1]
        keys_t = keys.T
        if is_outer(at_frame):
            chunks = [toks(near)]
        else:
            chunks = [pl.ds(at, 256) for at in range(0, 2 * tokens, 256)]

        all_probs, all_dscores = [], []
        for some in chunks:
            scores = jnp.dot(keys, turned[col, 0, :, some], preferred_element_type=jnp.float32)
            dprobs = jnp.dot(values, turned[col, 1, :, some], preferred_element_type=jnp.float32)
            probs = jnp.exp2(scores * (scale * LOG2E) - stat[col, 0:1, some])
            dscores = (probs * (dprobs - stat[col, 1:2, some])).astype(jnp.bfloat16)
            dq_sum[col, :, some] += jnp.dot(keys_t, dscores, preferred_element_type=jnp.float32)
            all_probs.append(probs.astype(jnp.bfloat16))
            all_dscores.append(dscores)
        together = chunks[0] if len(chunks) == 1 else pl.ds(0, 2 * tokens)
        dv = jnp.dot(
            jnp.concatenate(all_probs, axis=1), qd[col, 1, together, :], preferred_element_type=jnp.float32
        )
        dk = jnp.dot(
            jnp.concatenate(all_dscores, axis=1), qd[col, 0, together, :], preferred_element_type=jnp.float32
        )
        if first:
            sums[at_row, at_frame, 0] = dk
            sums[at_row, at_frame, 1] = dv
        else:
            sums[at_row, at_frame, 0] += dk
            sums[at_row, at_frame, 1] += dv

    def give_back(at_row, at_frame):
        grads_out[at_row, at_frame] = sums[at_row, at_frame].astype(jnp.bfloat16)
        remote(
            grads_out.at[at_row, at_frame], grads_in.at[2 - at_row, at_frame],
            ret_send.at[at_row, at_frame], ret_recv.at[2 - at_row, at_frame],
            (across_f if is_outer(at_frame) else f, r + at_row - 1, b),
        ).start()

    def q_arrived(col):
        for frame in range(2):
            for kind in range(3):
                arrived(q_slot(kind, frame, col), q_recv.at[col, frame, kind])
        for kind in range(2):
            turned[col, kind] = qd[col, kind].T

    def own_row(col, first):
        def body(frame, carry):
            one_block(1, frame, col, first)
            return carry

        lax.fori_loop(0, 2, body, 0)

    def both_sides(frame, wait, blocks, back):
        def body(side, carry):
            at_row = 2 * side
            to_row = r + at_row - 1

            @pl.when((to_row >= 0) & (to_row < rows))
            def _():
                if wait and is_outer(frame):
                    arrived(kv.at[at_row, 2, :, by_row], corner_recv.at[at_row, 0])
                    arrived(kv.at[at_row, 2, :, by_frame], corner_recv.at[at_row, 1])
                elif wait:
                    arrived(kv.at[at_row, frame], halo_recv.at[at_row, frame])
                for col, first in blocks:
                    one_block(at_row, frame, col, first)
                if back:
                    give_back(at_row, frame)

            return carry

        lax.fori_loop(0, 2, body, 0)

    def send_dq(frame, which):
        dq_out[:, toks(frame)] = dq_sum[1 - b, :, toks(frame)].astype(jnp.bfloat16)
        remote(
            dq_out.at[:, toks(frame)], dq_in.at[:, toks(frame)], dq_send.at[which], dq_recv.at[which],
            (f, r, 1 - b),
        ).start()

    far = 1 - near
    q_arrived(b)
    own_row(b, True)
    pass_corners()
    one_block(1, 2, b, True)
    both_sides(near, False, ((b, True),), False)
    q_arrived(1 - b)
    one_block(1, 2, 1 - b, False)
    give_back(1, 2)
    both_sides(near, False, ((1 - b, False),), True)
    both_sides(2, True, ((1 - b, True), (b, False)), True)
    own_row(1 - b, False)
    both_sides(far, True, ((1 - b, True),), False)
    send_dq(far, 0)
    send_dq(near, 1)
    both_sides(far, False, ((b, False),), True)

    def add_back(frame, at_row, at_frame):
        arrived(grads_in.at[at_row, at_frame], ret_recv.at[at_row, at_frame])
        sums[1, frame] += grads_in[at_row, at_frame].astype(jnp.float32)

    def finish_keys(frame):
        for step in (-1, 1):
            @pl.when(has_row[step])
            def _():
                add_back(frame, 1 + step, frame)

    def hand_out(kind, frame, src, ref):
        dst = ref.at[:, cols(a)]

        @pl.when(frame == a)
        def _():
            pltpu.make_async_copy(src, dst, out_recv.at[kind, a]).start()

        @pl.when(frame != a)
        def _():
            remote(src, dst, out_send.at[kind], out_recv.at[kind, a], (other_f, r, b)).start()

    def hand_out_keys(frame):
        final_kv[frame, 0] = (sums[1, frame, 0] * scale).astype(jnp.bfloat16)
        final_kv[frame, 1] = sums[1, frame, 1].astype(jnp.bfloat16)
        for kind, ref in ((1, dk_ref), (2, dv_ref)):
            hand_out(kind, frame, final_kv.at[frame, kind - 1], ref)

    def hand_out_queries(frame, which):
        arrived(dq_in.at[:, toks(frame)], dq_recv.at[which])
        total = dq_sum[b, :, toks(frame)] + dq_in[:, toks(frame)].astype(jnp.float32)
        final_q[toks(frame), :] = (total * scale).T.astype(jnp.bfloat16)
        hand_out(0, frame, final_q.at[toks(frame)], dq_ref)

    finish_keys(near)
    add_back(near, 1, 2)
    for step in (-1, 1):
        @pl.when(has_row[step])
        def _():
            add_back(near, 1 + step, 2)
    hand_out_keys(near)
    hand_out_queries(near, 1)
    hand_out_queries(far, 0)
    finish_keys(far)
    hand_out_keys(far)

    for kind in range(3):
        out = (dq_ref, dk_ref, dv_ref)[kind]
        for head in range(2):
            arrived(out.at[:, head * feats : (head + 1) * feats], out_recv.at[kind, head])
        arrived(final_kv.at[0, 0], out_send.at[kind])
        for which in range(3):
            arrived(q_source(kind, 0), q_send.at[which, kind])
    for which in range(2):
        arrived(kv.at[1, 0, which], kv_send.at[which])
        arrived(dq_out.at[:, toks(0)], dq_send.at[which])
    arrived(kv.at[1, 2], halo_send.at[1, 2])
    arrived(grads_out.at[1, 2], ret_send.at[1, 2])
    for step in (-1, 1):
        @pl.when(has_row[step])
        def _():
            arrived(kv.at[1, 2, :, by_row], halo_send.at[1 - step, 2])
            arrived(kv.at[1, 2, :, by_frame], corner_send.at[1 + step])
            for frame in range(2):
                arrived(kv.at[1 - step, frame], halo_send.at[1 - step, frame])
            for frame in range(3):
                arrived(grads_out.at[1 + step, frame], ret_send.at[1 + step, frame])


def copy_kernel(*refs):
    sems = refs[6]
    copies = [pltpu.make_async_copy(refs[at], refs[3 + at], sems.at[at]) for at in range(3)]
    for copy in copies:
        copy.start()
    for copy in copies:
        copy.wait()


def local_window(rows, queries, key_vectors, value_vectors, forward_out, cotangent, log_norm):
    shape = queries.shape
    tokens, width = shape[3:]
    feats = width // 2
    flat = [x.reshape(tokens, width) for x in (queries, key_vectors, value_vectors, forward_out, cotangent)]
    half = (tokens, feats)
    low, full = jnp.bfloat16, jnp.float32
    dma = pltpu.SemaphoreType.DMA
    any_space = pl.BlockSpec(memory_space=pl.ANY)
    vmem = pl.BlockSpec(memory_space=pltpu.VMEM)
    outs = pl.pallas_call(
        functools.partial(window_kernel, rows),
        out_shape=[jax.ShapeDtypeStruct((tokens, width), low)] * 3,
        in_specs=[any_space] * 6,
        out_specs=[any_space] * 3,
        scratch_shapes=[
            pltpu.VMEM((3, 3, 2) + half, low),
            pltpu.VMEM((2, 2, 2 * tokens, feats), low),
            pltpu.VMEM((2, 2, feats, 2 * tokens), low),
            pltpu.VMEM((2, 8, 2 * tokens), full),
            pltpu.VMEM((2, 8, tokens), full),
            pltpu.VMEM((tokens, width), low),
            pltpu.VMEM((tokens, width), low),
            pltpu.VMEM((2, tokens), full),
            pltpu.VMEM((3, 3, 2) + half, low),
            pltpu.VMEM((3, 3, 2) + half, low),
            pltpu.VMEM((3, 3, 2) + half, full),
            pltpu.VMEM((2, feats, 2 * tokens), full),
            pltpu.VMEM((feats, 2 * tokens), low),
            pltpu.VMEM((feats, 2 * tokens), low),
            pltpu.VMEM((2, 2) + half, low),
            pltpu.VMEM((2 * tokens, feats), low),
            dma((3,)), dma((2,)), dma((2, 2)), dma((3, 3)), dma((2, 2, 3)), dma((3, 3)), dma((3, 3)), dma((3,)), dma((3, 2)),
            dma((3, 3)), dma((3, 3)), dma((2,)), dma((2,)), dma((3,)), dma((3, 2)),
        ],
        compiler_params=pltpu.CompilerParams(
            collective_id=0, has_side_effects=True, vmem_limit_bytes=60 * 2**20
        ),
    )(*flat, log_norm.reshape(2, tokens))
    outs = pl.pallas_call(
        copy_kernel,
        out_shape=[jax.ShapeDtypeStruct((tokens, width), low)] * 3,
        in_specs=[vmem] * 3,
        out_specs=[any_space] * 3,
        scratch_shapes=[dma((3,))],
    )(*outs)
    return tuple(x.reshape(shape) for x in outs)


def solution(mesh):
    placed = (P("frame", "row", "col", None, None),) * 6
    sizes = dict(mesh.shape)
    body = local
    if sizes["frame"] == 4 and sizes["col"] == 2:
        body = functools.partial(local_window, sizes["row"])
    return jax.shard_map(
        body,
        mesh=mesh,
        in_specs=placed,
        out_specs=placed[:3],
        check_vma=False,
    )
```

```python
import functools

import jax
import jax.numpy as jnp
from jax import lax
from jax.experimental import pallas as pl
from jax.experimental.pallas import tpu as pltpu
from jax.sharding import PartitionSpec as P

MESH = pl.DeviceIdType.MESH
LOG2E = 1.4426950408889634


def passed_along(x, axis, by):
    peers = lax.axis_size(axis)
    pairs = [(i, i + by) for i in range(peers) if 0 <= i + by < peers]
    return lax.ppermute(x, axis, pairs)


def with_halo(x, sides, width):
    for axis, dim in sides:
        peers, length = (lax.axis_size(axis), x.shape[dim])
        up = [(i, (i + 1) % peers) for i in range(peers - 1)]
        down = [(j, i) for i, j in up]
        last = lax.slice_in_dim(x, length - width, length, axis=dim)
        leading = lax.slice_in_dim(x, 0, width, axis=dim)
        before = lax.ppermute(last, axis, up)
        after = lax.ppermute(leading, axis, down)
        x = jnp.concatenate([before, x, after], axis=dim)
    return x


def window_valid():
    offsets = jnp.arange(3, dtype=jnp.int32) - 1
    frame_pos = lax.axis_index("frame") + offsets
    row_pos = lax.axis_index("row") + offsets
    col_pos = lax.axis_index("col") + offsets
    along_f = (frame_pos >= 0) & (frame_pos < lax.axis_size("frame"))
    along_r = (row_pos >= 0) & (row_pos < lax.axis_size("row"))
    along_c = (col_pos >= 0) & (col_pos < lax.axis_size("col"))
    return along_f[:, None, None] & along_r[None, :, None] & along_c[None, None, :]


def reduce_frame(partial_sums, dim):
    from_next = passed_along(lax.index_in_dim(partial_sums, 0, dim, keepdims=False), "frame", -1)
    from_prev = passed_along(lax.index_in_dim(partial_sums, 2, dim, keepdims=False), "frame", 1)
    return lax.index_in_dim(partial_sums, 1, dim, keepdims=False) + from_next + from_prev


def reduce_row(partial_sums, dim):
    from_next = passed_along(lax.index_in_dim(partial_sums, 0, dim, keepdims=False), "row", -1)
    from_prev = passed_along(lax.index_in_dim(partial_sums, 2, dim, keepdims=False), "row", 1)
    return lax.index_in_dim(partial_sums, 1, dim, keepdims=False) + from_next + from_prev


def reduce_col(partial_sums, dim):
    from_next = passed_along(lax.index_in_dim(partial_sums, 0, dim, keepdims=False), "col", -1)
    from_prev = passed_along(lax.index_in_dim(partial_sums, 2, dim, keepdims=False), "col", 1)
    return lax.index_in_dim(partial_sums, 1, dim, keepdims=False) + from_next + from_prev


def fold_back(partial_sums):
    partial_sums = reduce_frame(partial_sums, 0)
    partial_sums = reduce_row(partial_sums, 0)
    return reduce_col(partial_sums, 0)


def local(queries, key_vectors, value_vectors, forward_out, cotangent, log_norm):
    tile_rows = queries.shape[3]
    width = queries.shape[4]
    head_count = log_norm.shape[3]
    head_width = width // head_count
    score_scale = head_width ** (-0.5)
    valid = window_valid().reshape(9, 3)
    own_q = queries.reshape(tile_rows, head_count, head_width)
    own_do = cotangent.reshape(tile_rows, head_count, head_width)
    products = cotangent.astype(jnp.float32) * forward_out.astype(jnp.float32)
    row_delta = jnp.sum(products.reshape(tile_rows, head_count, head_width), axis=-1).T
    own_log = log_norm.reshape(head_count, tile_rows)
    out_shape = (1, 1, 1, tile_rows, width)
    joined = jnp.concatenate((key_vectors, value_vectors), axis=3)
    nearby = with_halo(joined, (("frame", 0), ("row", 1), ("col", 2)), 1)
    nearby = nearby.reshape(9, 3, 2 * tile_rows, width)

    def slab_step(grad_q, inputs):
        slab, valid_slab = inputs
        near_k = slab[:, :tile_rows].reshape(3 * tile_rows, head_count, head_width)
        near_v = slab[:, tile_rows:].reshape(3 * tile_rows, head_count, head_width)
        keep = jnp.repeat(valid_slab, tile_rows)
        scores = (
            jnp.einsum("qhd,khd->hqk", own_q, near_k, preferred_element_type=jnp.float32)
            * score_scale
        )
        probs = jnp.where(keep[None, None, :], jnp.exp(scores - own_log[:, :, None]), 0.0)
        dprobs = jnp.einsum("qhd,khd->hqk", own_do, near_v, preferred_element_type=jnp.float32)
        dscores = (probs * (dprobs - row_delta[:, :, None])).astype(jnp.bfloat16)
        grad_q = grad_q + jnp.einsum(
            "hqk,khd->qhd", dscores, near_k, preferred_element_type=jnp.float32
        )
        grad_k = jnp.einsum("hqk,qhd->khd", dscores, own_q, preferred_element_type=jnp.float32)
        grad_v = jnp.einsum(
            "hqk,qhd->khd", probs.astype(jnp.bfloat16), own_do, preferred_element_type=jnp.float32
        )
        stacked = jnp.concatenate(
            (grad_k.reshape(3, tile_rows, width), grad_v.reshape(3, tile_rows, width)), axis=1
        )
        return (grad_q, stacked)

    zeros = jnp.zeros((tile_rows, head_count, head_width), jnp.float32)
    grad_q, partial_sums = lax.scan(slab_step, zeros, (nearby, valid))
    folded = fold_back(partial_sums.reshape(3, 3, 3, 2 * tile_rows, width))
    grad_queries = grad_q.reshape(tile_rows, width) * score_scale
    grad_keys = folded[:tile_rows] * score_scale
    grad_values = folded[tile_rows:]
    return (
        grad_queries.astype(jnp.bfloat16).reshape(out_shape),
        grad_keys.astype(jnp.bfloat16).reshape(out_shape),
        grad_values.astype(jnp.bfloat16).reshape(out_shape),
    )


def arrived(ref, sem):
    pltpu.make_async_copy(ref, ref, sem).wait()


def window_kernel(
    rows,
    q_ref, k_ref, v_ref, o_ref, do_ref, log_ref,
    dq_ref, dk_ref, dv_ref,
    kv, qd, turned, stat, stat_own, o_in, do_in, log_in, grads_out, grads_in, sums, dq_sum, dq_out, dq_in,
    final_kv, final_q,
    load_sem, kv_send, kv_recv, q_send, q_recv, halo_send, halo_recv, corner_send, corner_recv,
    ret_send, ret_recv, dq_send, dq_recv, out_send, out_recv,
):
    f, r, b = lax.axis_index("frame"), lax.axis_index("row"), lax.axis_index("col")
    y, a = f // 2, f % 2
    tokens, width = q_ref.shape
    feats = width // 2
    scale = feats ** (-0.5)
    other_f = 2 * y + 1 - a
    across_f = f + 2 - 4 * y
    near = 1 - y
    has_row = {-1: r > 0, 1: r < rows - 1}

    barrier = pltpu.get_barrier_semaphore()

    def greet(where):
        pl.semaphore_signal(barrier, inc=1, device_id=where, device_id_type=MESH)

    for where in ((other_f, r, b), (f, r, 1 - b), (other_f, r, 1 - b), (across_f, r, b)):
        greet(where)
    for step in (-1, 1):
        @pl.when(has_row[step])
        def _():
            greet((f, r + step, b))
            greet((across_f, r + step, b))

    def cols(head):
        return pl.ds(pl.multiple_of(head * feats, feats), feats)

    def toks(frame):
        return pl.ds(pl.multiple_of(frame * tokens, 128), tokens)

    def remote(src, dst, send, recv, where):
        return pltpu.make_async_remote_copy(
            src_ref=src, dst_ref=dst, send_sem=send, recv_sem=recv, device_id=where, device_id_type=MESH
        )

    def q_slot(kind, frame, col):
        if kind == 2:
            return stat.at[col, :, toks(frame)]
        return qd.at[col, kind, toks(frame)]

    def q_source(kind, head):
        if kind == 2:
            return stat_own.at[head]
        return (q_ref, do_ref)[kind].at[:, cols(head)]

    def q_local(kind):
        pltpu.make_async_copy(q_source(kind, a), q_slot(kind, a, b), q_recv.at[b, a, kind]).start()

    def q_remote(kind, which):
        head, col = ((1 - a, b), (a, 1 - b), (1 - a, 1 - b))[which]
        remote(
            q_source(kind, head), q_slot(kind, a, b), q_send.at[which, kind], q_recv.at[b, a, kind],
            (2 * y + head, r, col),
        ).start()

    loads = [
        pltpu.make_async_copy(src, dst, load_sem.at[at])
        for at, (src, dst) in enumerate(((do_ref, do_in), (o_ref, o_in), (log_ref, log_in)))
    ]
    for kind, ref in enumerate((k_ref, v_ref)):
        pltpu.make_async_copy(ref.at[:, cols(a)], kv.at[1, a, kind], kv_recv.at[a, kind]).start()
    for load in loads:
        load.start()
    for kind in range(2):
        q_local(kind)

    for load in loads:
        load.wait()
    ones = jnp.ones((8, feats), jnp.bfloat16)
    along = (((1,), (1,)), ((), ()))
    for head in range(2):
        part = slice(head * feats, (head + 1) * feats)
        product = do_in[:, part].astype(jnp.float32) * o_in[:, part].astype(jnp.float32)
        high = product.astype(jnp.bfloat16)
        low = (product - high.astype(jnp.float32)).astype(jnp.bfloat16)
        delta = lax.dot_general(ones, high, along, preferred_element_type=jnp.float32)
        delta += lax.dot_general(ones, low, along, preferred_element_type=jnp.float32)
        stat_own[head] = delta
        stat_own[head, 0:1, :] = log_in[head : head + 1, :] * LOG2E
    q_local(2)

    pl.semaphore_wait(
        barrier, 4 + 2 * (has_row[-1].astype(jnp.int32) + has_row[1].astype(jnp.int32))
    )

    for kind, ref in enumerate((k_ref, v_ref)):
        remote(
            ref.at[:, cols(1 - a)], kv.at[1, a, kind], kv_send.at[kind], kv_recv.at[a, kind], (other_f, r, b)
        ).start()
    for which in range(3):
        for kind in (2, 0, 1):
            q_remote(kind, which)

    for frame in (near, 1 - near):
        for kind in range(2):
            arrived(kv.at[1, frame, kind], kv_recv.at[frame, kind])
        if frame is near:
            remote(
                kv.at[1, frame], kv.at[1, 2], halo_send.at[1, 2], halo_recv.at[1, 2], (across_f, r, b)
            ).start()
        for step in (-1, 1):
            @pl.when(has_row[step])
            def _():
                remote(
                    kv.at[1, frame], kv.at[1 - step, frame], halo_send.at[1 - step, frame],
                    halo_recv.at[1 - step, frame], (f, r + step, b),
                ).start()

    dq_sum[...] = jnp.zeros_like(dq_sum)

    def is_outer(frame):
        return isinstance(frame, int) and frame == 2

    by_row, by_frame = pl.ds(0, tokens // 3), pl.ds(tokens // 3, tokens - tokens // 3)

    def pass_corners():
        arrived(kv.at[1, 2], halo_recv.at[1, 2])
        for step in (-1, 1):
            @pl.when(has_row[step])
            def _():
                remote(
                    kv.at[1, 2, :, by_row], kv.at[1 - step, 2, :, by_row], halo_send.at[1 - step, 2],
                    corner_recv.at[1 - step, 0], (f, r + step, b),
                ).start()
        for step in (-1, 1):
            @pl.when(has_row[step])
            def _():
                arrived(kv.at[1 + step, near], halo_recv.at[1 + step, near])
                remote(
                    kv.at[1 + step, near, :, by_frame], kv.at[1 + step, 2, :, by_frame],
                    corner_send.at[1 + step], corner_recv.at[1 + step, 1], (across_f, r, b),
                ).start()

    def one_block(at_row, at_frame, col, first):
        keys = kv[at_row, at_frame, 0]
        values = kv[at_row, at_frame, 1]
        keys_t = keys.T
        if is_outer(at_frame):
            chunks = [toks(near)]
        else:
            chunks = [pl.ds(at, 256) for at in range(0, 2 * tokens, 256)]

        all_probs, all_dscores = [], []
        for some in chunks:
            scores = jnp.dot(keys, turned[col, 0, :, some], preferred_element_type=jnp.float32)
            dprobs = jnp.dot(values, turned[col, 1, :, some], preferred_element_type=jnp.float32)
            probs = jnp.exp2(scores * (scale * LOG2E) - stat[col, 0:1, some])
            dscores = (probs * (dprobs - stat[col, 1:2, some])).astype(jnp.bfloat16)
            dq_sum[col, :, some] += jnp.dot(keys_t, dscores, preferred_element_type=jnp.float32)
            all_probs.append(probs.astype(jnp.bfloat16))
            all_dscores.append(dscores)
        together = chunks[0] if len(chunks) == 1 else pl.ds(0, 2 * tokens)
        dv = jnp.dot(
            jnp.concatenate(all_probs, axis=1), qd[col, 1, together, :], preferred_element_type=jnp.float32
        )
        dk = jnp.dot(
            jnp.concatenate(all_dscores, axis=1), qd[col, 0, together, :], preferred_element_type=jnp.float32
        )
        if first:
            sums[at_row, at_frame, 0] = dk
            sums[at_row, at_frame, 1] = dv
        else:
            sums[at_row, at_frame, 0] += dk
            sums[at_row, at_frame, 1] += dv

    def give_back(at_row, at_frame):
        grads_out[at_row, at_frame] = sums[at_row, at_frame].astype(jnp.bfloat16)
        remote(
            grads_out.at[at_row, at_frame], grads_in.at[2 - at_row, at_frame],
            ret_send.at[at_row, at_frame], ret_recv.at[2 - at_row, at_frame],
            (across_f if is_outer(at_frame) else f, r + at_row - 1, b),
        ).start()

    def q_arrived(col):
        for frame in range(2):
            for kind in range(3):
                arrived(q_slot(kind, frame, col), q_recv.at[col, frame, kind])
        for kind in range(2):
            turned[col, kind] = qd[col, kind].T

    def own_row(col, first):
        def body(frame, carry):
            one_block(1, frame, col, first)
            return carry

        lax.fori_loop(0, 2, body, 0)

    def both_sides(frame, wait, blocks, back):
        def body(side, carry):
            at_row = 2 * side
            to_row = r + at_row - 1

            @pl.when((to_row >= 0) & (to_row < rows))
            def _():
                if wait and is_outer(frame):
                    arrived(kv.at[at_row, 2, :, by_row], corner_recv.at[at_row, 0])
                    arrived(kv.at[at_row, 2, :, by_frame], corner_recv.at[at_row, 1])
                elif wait:
                    arrived(kv.at[at_row, frame], halo_recv.at[at_row, frame])
                for col, first in blocks:
                    one_block(at_row, frame, col, first)
                if back:
                    give_back(at_row, frame)

            return carry

        lax.fori_loop(0, 2, body, 0)

    def send_dq(frame, which):
        dq_out[:, toks(frame)] = dq_sum[1 - b, :, toks(frame)].astype(jnp.bfloat16)
        remote(
            dq_out.at[:, toks(frame)], dq_in.at[:, toks(frame)], dq_send.at[which], dq_recv.at[which],
            (f, r, 1 - b),
        ).start()

    far = 1 - near
    q_arrived(b)
    own_row(b, True)
    pass_corners()
    one_block(1, 2, b, True)
    both_sides(near, False, ((b, True),), False)
    q_arrived(1 - b)
    one_block(1, 2, 1 - b, False)
    give_back(1, 2)
    both_sides(near, False, ((1 - b, False),), True)
    both_sides(2, True, ((1 - b, True), (b, False)), True)
    own_row(1 - b, False)
    both_sides(far, True, ((1 - b, True),), False)
    send_dq(far, 0)
    send_dq(near, 1)
    both_sides(far, False, ((b, False),), True)

    def add_back(frame, at_row, at_frame):
        arrived(grads_in.at[at_row, at_frame], ret_recv.at[at_row, at_frame])
        sums[1, frame] += grads_in[at_row, at_frame].astype(jnp.float32)

    def finish_keys(frame):
        for step in (-1, 1):
            @pl.when(has_row[step])
            def _():
                add_back(frame, 1 + step, frame)

    def hand_out(kind, frame, src, ref):
        dst = ref.at[:, cols(a)]

        @pl.when(frame == a)
        def _():
            pltpu.make_async_copy(src, dst, out_recv.at[kind, a]).start()

        @pl.when(frame != a)
        def _():
            remote(src, dst, out_send.at[kind], out_recv.at[kind, a], (other_f, r, b)).start()

    def hand_out_keys(frame):
        final_kv[frame, 0] = (sums[1, frame, 0] * scale).astype(jnp.bfloat16)
        final_kv[frame, 1] = sums[1, frame, 1].astype(jnp.bfloat16)
        for kind, ref in ((1, dk_ref), (2, dv_ref)):
            hand_out(kind, frame, final_kv.at[frame, kind - 1], ref)

    def hand_out_queries(frame, which):
        arrived(dq_in.at[:, toks(frame)], dq_recv.at[which])
        total = dq_sum[b, :, toks(frame)] + dq_in[:, toks(frame)].astype(jnp.float32)
        final_q[toks(frame), :] = (total * scale).T.astype(jnp.bfloat16)
        hand_out(0, frame, final_q.at[toks(frame)], dq_ref)

    finish_keys(near)
    add_back(near, 1, 2)
    for step in (-1, 1):
        @pl.when(has_row[step])
        def _():
            add_back(near, 1 + step, 2)
    hand_out_keys(near)
    hand_out_queries(near, 1)
    hand_out_queries(far, 0)
    finish_keys(far)
    hand_out_keys(far)

    for kind in range(3):
        out = (dq_ref, dk_ref, dv_ref)[kind]
        for head in range(2):
            arrived(out.at[:, head * feats : (head + 1) * feats], out_recv.at[kind, head])
        arrived(final_kv.at[0, 0], out_send.at[kind])
        for which in range(3):
            arrived(q_source(kind, 0), q_send.at[which, kind])
    for which in range(2):
        arrived(kv.at[1, 0, which], kv_send.at[which])
        arrived(dq_out.at[:, toks(0)], dq_send.at[which])
    arrived(kv.at[1, 2], halo_send.at[1, 2])
    arrived(grads_out.at[1, 2], ret_send.at[1, 2])
    for step in (-1, 1):
        @pl.when(has_row[step])
        def _():
            arrived(kv.at[1, 2, :, by_row], halo_send.at[1 - step, 2])
            arrived(kv.at[1, 2, :, by_frame], corner_send.at[1 + step])
            for frame in range(2):
                arrived(kv.at[1 - step, frame], halo_send.at[1 - step, frame])
            for frame in range(3):
                arrived(grads_out.at[1 + step, frame], ret_send.at[1 + step, frame])


def copy_kernel(*refs):
    held, sems = refs[6], refs[7]
    loads = [pltpu.make_async_copy(refs[at], held.at[at], sems.at[at]) for at in range(3)]
    stores = [pltpu.make_async_copy(held.at[at], refs[3 + at], sems.at[3 + at]) for at in range(3)]
    for load in loads:
        load.start()
    for load, store in zip(loads, stores):
        load.wait()
        store.start()
    for store in stores:
        store.wait()


def local_window(rows, queries, key_vectors, value_vectors, forward_out, cotangent, log_norm):
    shape = queries.shape
    tokens, width = shape[3:]
    feats = width // 2
    flat = [x.reshape(tokens, width) for x in (queries, key_vectors, value_vectors, forward_out, cotangent)]
    half = (tokens, feats)
    low, full = jnp.bfloat16, jnp.float32
    dma = pltpu.SemaphoreType.DMA
    any_space = pl.BlockSpec(memory_space=pl.ANY)
    outs = pl.pallas_call(
        functools.partial(window_kernel, rows),
        out_shape=[jax.ShapeDtypeStruct((tokens, width), low)] * 3,
        in_specs=[any_space] * 6,
        out_specs=[any_space] * 3,
        scratch_shapes=[
            pltpu.VMEM((3, 3, 2) + half, low),
            pltpu.VMEM((2, 2, 2 * tokens, feats), low),
            pltpu.VMEM((2, 2, feats, 2 * tokens), low),
            pltpu.VMEM((2, 8, 2 * tokens), full),
            pltpu.VMEM((2, 8, tokens), full),
            pltpu.VMEM((tokens, width), low),
            pltpu.VMEM((tokens, width), low),
            pltpu.VMEM((2, tokens), full),
            pltpu.VMEM((3, 3, 2) + half, low),
            pltpu.VMEM((3, 3, 2) + half, low),
            pltpu.VMEM((3, 3, 2) + half, full),
            pltpu.VMEM((2, feats, 2 * tokens), full),
            pltpu.VMEM((feats, 2 * tokens), low),
            pltpu.VMEM((feats, 2 * tokens), low),
            pltpu.VMEM((2, 2) + half, low),
            pltpu.VMEM((2 * tokens, feats), low),
            dma((3,)), dma((2,)), dma((2, 2)), dma((3, 3)), dma((2, 2, 3)), dma((3, 3)), dma((3, 3)), dma((3,)), dma((3, 2)),
            dma((3, 3)), dma((3, 3)), dma((2,)), dma((2,)), dma((3,)), dma((3, 2)),
        ],
        compiler_params=pltpu.CompilerParams(
            collective_id=0, has_side_effects=True, vmem_limit_bytes=60 * 2**20
        ),
    )(*flat, log_norm.reshape(2, tokens))
    outs = pl.pallas_call(
        copy_kernel,
        out_shape=[jax.ShapeDtypeStruct((tokens, width), low)] * 3,
        in_specs=[any_space] * 3,
        out_specs=[any_space] * 3,
        scratch_shapes=[pltpu.VMEM((3, tokens, width), low), dma((6,))],
    )(*outs)
    return tuple(x.reshape(shape) for x in outs)


def solution(mesh):
    placed = (P("frame", "row", "col", None, None),) * 6
    sizes = dict(mesh.shape)
    body = local
    if sizes["frame"] == 4 and sizes["col"] == 2:
        body = functools.partial(local_window, sizes["row"])
    return jax.shard_map(
        body,
        mesh=mesh,
        in_specs=placed,
        out_specs=placed[:3],
        check_vma=False,
    )
```
